32 devices in a mesh: replica: 4 (over y, core), shard: 8 (over z, x).
Axes of the slice: x: 2, y: 2, z: 4, core: 2. Of those that a mesh axis runs over, the one named last changes fastest.
Arguments:
- tokens_in: bfloat16 [4096, 8192], P(('replica', 'shard')), may hold values from -6 to 6
- cotangent: bfloat16 [4096, 128], P(('replica', 'shard')), may hold values from -0.1875 to 0.1875
- next_tokens: bfloat16 [2048, 8192], P(('replica', 'shard')), may hold values from -6 to 6
- master: float32 [8192, 128], P(('replica', 'shard')), may hold values from -0.0625 to 0.0625
- first_moment: float32 [8192, 128], P(('replica', 'shard')), may hold values from -6 to 6
- second_moment: float32 [8192, 128], P(('replica', 'shard')), may hold values from 0.25 to 4
Outputs:
- new_master: float32 [8192, 128], P(('replica', 'shard'))
- new_first: float32 [8192, 128], P(('replica', 'shard'))
- new_second: float32 [8192, 128], P(('replica', 'shard'))
- next_out: bfloat16 [2048, 128], P(('replica', 'shard'))
The draws below stay inside these ranges and needn't reach their ends.
All inputs are finite; a program needn't handle non-finite values.
Results may differ from the reference program's by a relative error of at most 0.005.
Values may be sent and summed in bfloat16 or wider, within the bound.
A program may use at most 64 MiB of HBM per device.

```python
import math
import jax
import jax.numpy as jnp
from jax import lax

D = 8192
COLS = 128
TOKENS = 4096
NEXT_TOKENS = 2048


def raised(entries, stream_key, source, target, blocks, factor):
    owner, partner = [(jnp.arange(entries.shape[position]) // (entries.shape[position] // blocks)).reshape([-1 if axis == position else 1 for axis in range(entries.ndim)]) for position in (source, target)]
    chosen = jax.random.permutation(stream_key, blocks)[partner]
    strong = (owner == chosen) | (owner == (partner + blocks // 2) % blocks)
    return jnp.where(strong, factor * entries, entries)


def shard_levels(own_key, dims, cuts, least, top_value):
    level = 1.0
    for dim, shards_of in cuts:
        heights = jax.random.uniform(jax.random.fold_in(jax.random.fold_in(own_key, 6), dim), (shards_of,), jnp.float32, least / len(cuts), top_value / len(cuts))
        level = level * jnp.repeat(jnp.exp(heights), dims[dim] // shards_of).reshape((-1,) + (1,) * (len(dims) - 1 - dim))
    return level


def gaussian(key, dims, deviation, reach, pieces=(), kind=jnp.bfloat16):
    entries = jax.random.normal(key, dims, jnp.float32) * deviation
    if len(pieces) > 0:
        entries = shard_levels(key, dims, pieces, -0.22, 0.18) * entries
    return jnp.clip(entries, min=-reach, max=reach).astype(kind)


def gaussian_with(own_key, dims, deviation, reach, pieces, heavy, kind=jnp.bfloat16):
    result = deviation * jax.random.normal(own_key, dims, jnp.float32)
    if pieces:
        result = result * shard_levels(own_key, dims, pieces, -0.22, 0.18)
    return jnp.clip(raised(result, jax.random.fold_in(own_key, 3), *heavy), -reach, reach).astype(kind)


def setup_inputs(seed: int = 0) -> dict:
    keys = jax.random.split(jax.random.key(seed), 7)
    tokens_in = gaussian_with(keys[0], (TOKENS, D), 1.0, 6.0, ((0, 32),), (0, 1, 32, 2.75))
    cotangent = gaussian(keys[1], (TOKENS, COLS), (2.0 / (TOKENS ** 0.5)), 0.1875, ((0, 32),))
    next_tokens = gaussian_with(keys[2], (NEXT_TOKENS, D), 1.0, 6.0, ((0, 32),), (0, 1, 32, 2.75))
    master = gaussian(keys[3], (D, COLS), D ** -0.5, 0.0625, ((0, 32),), jnp.float32)
    first_moment = gaussian(keys[4], (D, COLS), 1.0, 6.0, ((0, 32),), jnp.float32)
    second_moment = jnp.clip(jnp.exp(math.log(4.0) - 2.7725887 * jax.random.uniform(keys[5], (D, COLS), jnp.float32) ** shard_levels(keys[5], (D, COLS), ((0, 32),), -0.2, 0.2)), 0.25, 4.0)
    return dict(tokens_in=tokens_in, cotangent=cotangent, next_tokens=next_tokens, master=master, first_moment=first_moment, second_moment=second_moment)


beta_one = 0.9
beta_two = 0.95
learn_rate = 0.003
decay_rate = 0.1
epsilon = 1e-08
steps_done = 10

def reference(tokens_in, cotangent, next_tokens, master, first_moment, second_moment):
    gradient = lax.dot_general(tokens_in, cotangent, (((0,), (0,)), ((), ())), preferred_element_type=jnp.float32)
    new_first = beta_one * first_moment + (1.0 - beta_one) * gradient
    new_second = beta_two * second_moment + (1.0 - beta_two) * gradient * gradient
    first_hat = new_first / (1.0 - beta_one ** steps_done)
    second_hat = new_second / (1.0 - beta_two ** steps_done)
    new_master = master - learn_rate * (first_hat / (jnp.sqrt(second_hat) + epsilon) + decay_rate * master)
    low_weight = new_master.astype(jnp.bfloat16)
    next_out = jnp.dot(next_tokens, low_weight, preferred_element_type=jnp.float32).astype(jnp.bfloat16)
    return (new_master, new_first, new_second, next_out)
```

```python
import functools

import jax
import jax.numpy as jnp
from jax import lax
from jax.experimental import pallas as pl
from jax.experimental.pallas import tpu as pltpu
from jax.sharding import PartitionSpec as P

beta_one = 0.9
beta_two = 0.95
learn_rate = 0.003
decay_rate = 0.1
epsilon = 1e-08
steps_done = 10

MESH = pl.DeviceIdType.MESH
PAIR = 2


def adam(gradient, master, first_moment, second_moment):
    new_first = beta_one * first_moment + (1.0 - beta_one) * gradient
    new_second = beta_two * second_moment + (1.0 - beta_two) * gradient * gradient
    first_hat = new_first / (1.0 - beta_one**steps_done)
    second_hat = new_second / (1.0 - beta_two**steps_done)
    new_master = master - learn_rate * (
        first_hat / (jnp.sqrt(second_hat) + epsilon) + decay_rate * master
    )
    return new_master, new_first, new_second


def kernel(
    Z, own,
    tok_hbm, cot_hbm, nxt_hbm, master_hbm, first_hbm, second_hbm,
    nm_hbm, nf_hbm, ns_hbm, out_ref,
    tok, cot, nxt, state, fresh,
    g32, gb, rc, hb, rp, jb, rq, kb, rz, wall, acc, ro,
    tok_sem, cot_sem, nxt_sem, state_sem, fresh_sem,
    swap_s, swap_r, c_s, c_r, p_s, p_r, q_s, q_r, z_s, z_r,
    az_s, az_r, aq_s, aq_r, ap_s, ap_r, o_s, o_r,
):
    f32, bf16 = jnp.float32, jnp.bfloat16
    r, s = lax.axis_index("replica"), lax.axis_index("shard")
    y, c, z, x = r // PAIR, r % PAIR, s // PAIR, s % PAIR
    p, q = x * (1 - c) + y * c, y * (1 - c) + x * c
    wide = PAIR * own
    half_cols = Z * wide

    def at(yy, cc, zz, xx):
        return (yy * PAIR + cc, zz * PAIR + xx)

    sib = at(y, 1 - c, z, x)
    p_peer = at(y * (1 - c) + (1 - y) * c, c, z, (1 - x) * (1 - c) + x * c)
    q_peer = at((1 - y) * (1 - c) + y * c, c, z, x * (1 - c) + (1 - x) * c)

    def z_at(j):
        return at(y, c, (z + j) % Z, x)

    loads = []
    cot_load = pltpu.make_async_copy(cot_hbm, cot, cot_sem)
    cot_load.start()
    for k in range(Z):
        zc = (z + 1 + k) % Z
        row = []
        for yc in range(PAIR * PAIR):
            col = pl.multiple_of((yc * Z + zc) * wide, own)
            cp = pltpu.make_async_copy(
                tok_hbm.at[:, pl.ds(col, wide)], tok.at[k, yc], tok_sem.at[k, yc]
            )
            cp.start()
            row.append(cp)
        loads.append(row)

    barrier = pltpu.get_barrier_semaphore()
    peers = [sib, p_peer, q_peer] + [z_at(j) for j in range(1, Z)]
    for d in peers:
        pl.semaphore_signal(barrier, inc=1, device_id=d, device_id_type=MESH)

    state_loads = [
        pltpu.make_async_copy(src, state.at[i], state_sem.at[i])
        for i, src in enumerate((master_hbm, first_hbm, second_hbm))
    ]
    rows = nxt_hbm.shape[0]
    nxt_loads = []
    for yy in range(PAIR):
        col = pl.multiple_of((yy * PAIR + c) * half_cols, own)
        nxt_loads.append(
            pltpu.make_async_copy(
                nxt_hbm.at[:, pl.ds(col, half_cols)], nxt.at[yy, pl.ds(0, rows)], nxt_sem.at[yy]
            )
        )
    for cp in state_loads + nxt_loads:
        cp.start()

    def send(src, dst, s_sem, r_sem, dev):
        cp = pltpu.make_async_remote_copy(
            src_ref=src, dst_ref=dst, send_sem=s_sem, recv_sem=r_sem,
            device_id=dev, device_id_type=MESH,
        )
        cp.start()
        return cp

    sent = []
    cot_load.wait()
    cot_t = cot[...].astype(f32).T.astype(bf16)
    core_cp, p_cp, q_cp, z_cp, swaps = {}, {}, {}, {}, []

    def compute(k):
        for cp in loads[k]:
            cp.wait()
        for yy in range(PAIR):
            for h in range(PAIR):
                for xx in range(PAIR):
                    pp, qq = (xx, yy) if h == 0 else (yy, xx)
                    block = jnp.dot(
                        cot_t, tok[k, yy * PAIR + h, :, xx * own:(xx + 1) * own],
                        preferred_element_type=f32,
                    )
                    g32[k, h, pp, qq] = block
                    gb[k, h, pp, qq] = block.astype(bf16)

    def stage_core(k):
        core_cp[k] = send(gb.at[k, 1 - c], rc.at[k], c_s.at[k], c_r.at[k], sib)

    def stage_p(k):
        core_cp[k].wait_recv()
        for qq in range(PAIR):
            hb[k, qq] = (g32[k, c, 1 - p, qq] + rc[k, 1 - p, qq].astype(f32)).astype(bf16)
        p_cp[k] = send(hb.at[k], rp.at[k], p_s.at[k], p_r.at[k], p_peer)

    def partial(k, qq):
        return g32[k, c, p, qq] + rc[k, p, qq].astype(f32) + rp[k, qq].astype(f32)

    def stage_q(k):
        p_cp[k].wait_recv()
        jb[k] = partial(k, 1 - q).astype(bf16)
        q_cp[k] = send(jb.at[k], rq.at[k], q_s.at[k], q_r.at[k], q_peer)

    def stage_z(k):
        q_cp[k].wait_recv()
        total = partial(k, q) + rq[k].astype(f32)
        if k == Z - 1:
            return total
        kb[k] = total.astype(bf16)
        z_cp[k] = send(kb.at[k], rz.at[k], z_s.at[k], z_r.at[k], z_at(k + 1))
        return None

    total = None
    for t in range(Z + 3):
        if t < Z:
            compute(t)
            if t == 0:
                pl.semaphore_wait(barrier, len(peers))
            stage_core(t)
            if t == Z - 1:
                for yy in range(PAIR):
                    col = pl.multiple_of((yy * PAIR + 1 - c) * half_cols, own)
                    swaps.append(
                        send(
                            nxt_hbm.at[:, pl.ds(col, half_cols)], nxt.at[yy, pl.ds(rows, rows)],
                            swap_s.at[yy], swap_r.at[yy], sib,
                        )
                    )
        if 0 <= t - 1 < Z:
            stage_p(t - 1)
        if 0 <= t - 2 < Z:
            stage_q(t - 2)
        if 0 <= t - 3 < Z:
            total = stage_z(t - 3)

    for k in range(Z - 1):
        z_cp[k].wait_recv()
        total = total + rz[k].astype(f32)
    for cp in state_loads:
        cp.wait()
    new_master, new_first, new_second = adam(total.T, state[0], state[1], state[2])
    wall[z, p, q] = new_master.astype(bf16)

    az, aq, ap = {}, {}, {}
    for j in range(1, Z):
        az[j] = send(
            wall.at[z, p, q], wall.at[z, p, q], az_s.at[j - 1], az_r.at[j - 1], z_at(j)
        )

    def forward(j):
        zj = (z - j + Z) % Z
        aq[j] = send(wall.at[zj, p, q], wall.at[zj, p, q], aq_s.at[j], aq_r.at[j], q_peer)
        ap[j, 0] = send(
            wall.at[zj, p, q], wall.at[zj, p, q], ap_s.at[j, 0], ap_r.at[j, 0], p_peer
        )

    def forward_second(j):
        zj = (z - j + Z) % Z
        aq[j].wait_recv()
        ap[j, 1] = send(
            wall.at[zj, p, 1 - q], wall.at[zj, p, 1 - q], ap_s.at[j, 1], ap_r.at[j, 1], p_peer
        )

    def product(j, pp, qq):
        zj = (z - j + Z) % Z
        yy, xx = qq * (1 - c) + pp * c, pp * (1 - c) + qq * c
        col = pl.multiple_of((zj * PAIR + xx) * own, own)
        return jnp.dot(
            nxt[yy, :, pl.ds(col, own)], wall[zj, pp, qq], preferred_element_type=f32
        )

    forward(0)
    for i, value in enumerate((new_master, new_first, new_second)):
        fresh[i] = value
    stores = [
        pltpu.make_async_copy(fresh.at[i], dst, fresh_sem.at[i])
        for i, dst in enumerate((nm_hbm, nf_hbm, ns_hbm))
    ]
    for cp in stores:
        cp.start()
    for cp in nxt_loads:
        cp.wait()
    for cp in swaps:
        cp.wait_recv()
    acc[...] = product(0, p, q)
    for j in range(1, Z):
        az[j].wait_recv()
        forward(j)
        forward_second(j - 1)
        acc[...] += product(j, p, q) + product(j - 1, p, 1 - q)
        ap[j - 1, 0].wait_recv()
        acc[...] += product(j - 1, 1 - p, q)
    forward_second(Z - 1)
    acc[...] += product(Z - 1, p, 1 - q)
    for j in range(Z - 1):
        ap[j, 1].wait_recv()
        acc[...] += product(j, 1 - p, 1 - q)
    ap[Z - 1, 0].wait_recv()
    acc[...] += product(Z - 1, 1 - p, q)
    ap[Z - 1, 1].wait_recv()
    acc[...] += product(Z - 1, 1 - p, 1 - q)

    last = send(acc.at[pl.ds(rows, rows)], ro, o_s, o_r, sib)
    for cps in (core_cp, p_cp, q_cp, z_cp, az, aq, ap):
        for cp in cps.values():
            cp.wait_send()
    for cp in swaps:
        cp.wait_send()
    for cp in stores:
        cp.wait()
    last.wait_recv()
    out_ref[...] = (acc[pl.ds(0, rows)] + ro[...]).astype(bf16)
    last.wait_send()


def fused(Z, tokens_in, cotangent, next_tokens, master, first_moment, second_moment):
    f32, bf16 = jnp.float32, jnp.bfloat16
    own, cols = master.shape
    count = tokens_in.shape[0]
    rows = next_tokens.shape[0]
    dma = pltpu.SemaphoreType.DMA
    block = (cols, own)
    any_spec = pl.BlockSpec(memory_space=pl.ANY)
    scratch = [
        pltpu.VMEM((Z, PAIR * PAIR, count, PAIR * own), bf16),
        pltpu.VMEM((count, cols), bf16),
        pltpu.VMEM((PAIR, 2 * rows, Z * PAIR * own), bf16),
        pltpu.VMEM((3, own, cols), f32),
        pltpu.VMEM((3, own, cols), f32),
        pltpu.VMEM((Z, PAIR, PAIR, PAIR) + block, f32),
        pltpu.VMEM((Z, PAIR, PAIR, PAIR) + block, bf16),
        pltpu.VMEM((Z, PAIR, PAIR) + block, bf16),
        pltpu.VMEM((Z, PAIR) + block, bf16),
        pltpu.VMEM((Z, PAIR) + block, bf16),
        pltpu.VMEM((Z,) + block, bf16),
        pltpu.VMEM((Z,) + block, bf16),
        pltpu.VMEM((Z - 1,) + block, bf16),
        pltpu.VMEM((Z - 1,) + block, bf16),
        pltpu.VMEM((Z, PAIR, PAIR, own, cols), bf16),
        pltpu.VMEM((2 * rows, cols), f32),
        pltpu.VMEM((rows, cols), f32),
        dma((Z, PAIR * PAIR)), dma, dma((PAIR,)), dma((3,)), dma((3,)),
        dma((PAIR,)), dma((PAIR,)),
        dma((Z,)), dma((Z,)), dma((Z,)), dma((Z,)), dma((Z,)), dma((Z,)),
        dma((Z - 1,)), dma((Z - 1,)),
        dma((Z - 1,)), dma((Z - 1,)), dma((Z,)), dma((Z,)), dma((Z, 2)), dma((Z, 2)),
        dma, dma,
    ]
    return pl.pallas_call(
        functools.partial(kernel, Z, own),
        out_shape=(
            jax.ShapeDtypeStruct(master.shape, f32),
            jax.ShapeDtypeStruct(master.shape, f32),
            jax.ShapeDtypeStruct(master.shape, f32),
            jax.ShapeDtypeStruct((rows, cols), bf16),
        ),
        in_specs=[any_spec] * 6,
        out_specs=(any_spec, any_spec, any_spec, pl.BlockSpec(memory_space=pltpu.VMEM)),
        scratch_shapes=scratch,
        compiler_params=pltpu.CompilerParams(
            collective_id=0, has_side_effects=True, vmem_limit_bytes=32 * 2**20
        ),
    )(tokens_in, cotangent, next_tokens, master, first_moment, second_moment)


def plain(tokens_in, cotangent, next_tokens, master, first_moment, second_moment):
    n_rep = lax.axis_size("replica")
    n_shard = lax.axis_size("shard")
    model_width = tokens_in.shape[1]
    own_rows = model_width // (n_rep * n_shard)
    blocked = lax.psum_scatter(
        lax.dot_general(
            tokens_in, cotangent, (((0,), (0,)), ((), ())), preferred_element_type=jnp.float32
        ),
        "replica",
        scatter_dimension=0,
        tiled=True,
    )
    gradient = lax.psum_scatter(blocked, "shard", scatter_dimension=0, tiled=True)
    new_master, new_first, new_second = adam(gradient, master, first_moment, second_moment)
    low_weight = new_master.astype(jnp.bfloat16)
    group_rows = lax.all_gather(low_weight, "replica", axis=0, tiled=True)
    row_count = next_tokens.shape[0]
    arranged = next_tokens.reshape(row_count, n_rep, n_shard, own_rows).transpose(0, 2, 1, 3)
    columns = arranged.reshape(row_count, model_width)
    summed = jnp.dot(
        columns,
        lax.all_gather(group_rows, "shard", axis=0, tiled=True),
        preferred_element_type=jnp.float32,
    )
    return (new_master, new_first, new_second, summed.astype(jnp.bfloat16))


def solution(mesh):
    n_rep, n_shard = mesh.shape["replica"], mesh.shape["shard"]

    def on_device(tokens_in, cotangent, next_tokens, master, first_moment, second_moment):
        own, cols = master.shape
        fits = (
            n_rep == PAIR * PAIR
            and n_shard % PAIR == 0
            and n_shard > PAIR
            and own % 128 == 0
            and cols % 128 == 0
            and next_tokens.shape[0] % 16 == 0
            and tokens_in.shape[0] % 128 == 0
        )
        args = (tokens_in, cotangent, next_tokens, master, first_moment, second_moment)
        if fits:
            return tuple(fused(n_shard // PAIR, *args))
        return plain(*args)

    spec = P(("replica", "shard"), None)
    return jax.shard_map(
        on_device, mesh=mesh, in_specs=(spec,) * 6, out_specs=(spec,) * 4, check_vma=False
    )
```

```python
import functools

import jax
import jax.numpy as jnp
from jax import lax
from jax.experimental import pallas as pl
from jax.experimental.pallas import tpu as pltpu
from jax.sharding import PartitionSpec as P

beta_one = 0.9
beta_two = 0.95
learn_rate = 0.003
decay_rate = 0.1
epsilon = 1e-08
steps_done = 10

MESH = pl.DeviceIdType.MESH
PAIR = 2
VMEM_BYTES = 62 * 2**20


def adam(gradient, master, first_moment, second_moment):
    new_first = beta_one * first_moment + (1.0 - beta_one) * gradient
    new_second = beta_two * second_moment + (1.0 - beta_two) * gradient * gradient
    first_hat = new_first / (1.0 - beta_one**steps_done)
    second_hat = new_second / (1.0 - beta_two**steps_done)
    new_master = master - learn_rate * (
        first_hat / (jnp.sqrt(second_hat) + epsilon) + decay_rate * master
    )
    return new_master, new_first, new_second


def kernel(
    Z, own,
    tok_hbm, cot_hbm, nxt_hbm, master_hbm, first_hbm, second_hbm,
    nm_out, nf_out, ns_out, out_ref,
    tok, cot, nxt, state, fresh,
    g32, gb, rc, hb, rp, jb, rq, kb, rz, wall, acc, ro,
    tok_sem, cot_sem, nxt_sem, state_sem, fresh_sem,
    n_s, n_r, c_s, c_r, p_s, p_r, q_s, q_r, z_s, z_r,
    az_s, az_r, aq_s, aq_r, o_s, o_r,
):
    f32, bf16 = jnp.float32, jnp.bfloat16
    r, s = lax.axis_index("replica"), lax.axis_index("shard")
    y, c, z, x = r // PAIR, r % PAIR, s // PAIR, s % PAIR
    p, q = x * (1 - c) + y * c, y * (1 - c) + x * c
    wide = PAIR * own
    rows = nxt_hbm.shape[0]

    def at(yy, cc, zz, xx):
        return (yy * PAIR + cc, zz * PAIR + xx)

    def over_p(cc):
        return at(y * (1 - c) + (1 - y) * c, cc, z, (1 - x) * (1 - c) + x * c)

    def over_q(cc):
        return at((1 - y) * (1 - c) + y * c, cc, z, x * (1 - c) + (1 - x) * c)

    def z_at(j):
        return at(y, c, (z + j) % Z, x)

    def block_at(h, pp, qq, zz):
        yy, xx = qq * (1 - h) + pp * h, pp * (1 - h) + qq * h
        return ((yy * PAIR + h) * Z + zz) * PAIR + xx

    sib, p_peer, q_peer = at(y, 1 - c, z, x), over_p(c), over_q(c)

    loads = []
    cot_load = pltpu.make_async_copy(cot_hbm, cot, cot_sem)
    cot_load.start()
    for k in range(Z):
        zc = (z + 1 + k) % Z
        row = []
        for yc in range(PAIR * PAIR):
            col = pl.multiple_of((yc * Z + zc) * wide, own)
            cp = pltpu.make_async_copy(
                tok_hbm.at[:, pl.ds(col, wide)], tok.at[k, yc], tok_sem.at[k, yc]
            )
            cp.start()
            row.append(cp)
        loads.append(row)
        if k == 0:
            barrier = pltpu.get_barrier_semaphore()
            peers = [sib, p_peer, q_peer, over_p(1 - c), over_q(1 - c)]
            peers += [z_at(j) for j in range(1, Z)]
            for d in peers:
                pl.semaphore_signal(barrier, inc=1, device_id=d, device_id_type=MESH)

    def send(src, dst, s_sem, r_sem, dev):
        cp = pltpu.make_async_remote_copy(
            src_ref=src, dst_ref=dst, send_sem=s_sem, recv_sem=r_sem,
            device_id=dev, device_id_type=MESH,
        )
        cp.start()
        return cp

    cot_load.wait()
    cot_t = cot[...].astype(f32).T.astype(bf16)
    core_cp, p_cp, q_cp, z_cp = {}, {}, {}, {}

    def term(k, h, yy, xx):
        return jnp.dot(
            cot_t, tok[k, yy * PAIR + h, :, xx * own:(xx + 1) * own],
            preferred_element_type=f32,
        )

    def place(h, yy, xx):
        return xx * (1 - h) + yy * h, yy * (1 - h) + xx * h

    def stage_core(k):
        for cp in loads[k]:
            cp.wait()
        for yy in range(PAIR):
            for xx in range(PAIR):
                gb[(k,) + place(1 - c, yy, xx)] = term(k, 1 - c, yy, xx).astype(bf16)
        if k == 0:
            pl.semaphore_wait(barrier, len(peers))
        core_cp[k] = send(gb.at[k], rc.at[k], c_s.at[k], c_r.at[k], sib)

    def own_terms(k):
        for yy in range(PAIR):
            for xx in range(PAIR):
                g32[(k,) + place(c, yy, xx)] = term(k, c, yy, xx)

    def stage_p(k):
        core_cp[k].wait_recv()
        for qq in range(PAIR):
            hb[k, qq] = (g32[k, 1 - p, qq] + rc[k, 1 - p, qq].astype(f32)).astype(bf16)
        p_cp[k] = send(hb.at[k], rp.at[k], p_s.at[k], p_r.at[k], p_peer)

    def partial(k, qq):
        return g32[k, p, qq] + rc[k, p, qq].astype(f32) + rp[k, qq].astype(f32)

    def stage_q(k):
        p_cp[k].wait_recv()
        jb[k] = partial(k, 1 - q).astype(bf16)
        q_cp[k] = send(jb.at[k], rq.at[k], q_s.at[k], q_r.at[k], q_peer)

    def stage_z(k):
        q_cp[k].wait_recv()
        total = partial(k, q) + rq[k].astype(f32)
        if k == Z - 1:
            return total
        kb[k] = total.astype(bf16)
        z_cp[k] = send(kb.at[k], rz.at[k], z_s.at[k], z_r.at[k], z_at(k + 1))
        return None

    swaps, nxt_loads = {}, {}

    def swap(i, who):
        h, pp, qq, dev = (
            (1 - c, q, p, sib), (c, 1 - p, q, p_peer), (1 - c, 1 - q, p, over_q(1 - c))
        )[who]
        qq = qq if i == 0 else 1 - qq
        for j in range(Z):
            zj = (z - j + Z) % Z
            col = pl.multiple_of(block_at(h, pp, qq, zj) * own, own)
            swaps[i, who, j] = send(
                nxt_hbm.at[:, pl.ds(col, own)], nxt.at[zj, qq, pl.ds((who + 1) * rows, rows)],
                n_s.at[i, who, j], n_r.at[i, who, j], dev,
            )

    def local_tokens():
        for i in range(PAIR):
            qq = q if i == 0 else 1 - q
            for j in range(Z):
                zj = (z - j + Z) % Z
                col = pl.multiple_of(block_at(c, p, qq, zj) * own, own)
                cp = pltpu.make_async_copy(
                    nxt_hbm.at[:, pl.ds(col, own)], nxt.at[zj, qq, pl.ds(0, rows)], nxt_sem.at[i, j]
                )
                cp.start()
                nxt_loads[i, j] = cp

    state_loads = [
        pltpu.make_async_copy(src, state.at[i], state_sem.at[i])
        for i, src in enumerate((master_hbm, first_hbm, second_hbm))
    ]
    total = None
    for t in range(Z + 3):
        if t < Z:
            stage_core(t)
            if t == 0:
                swap(0, 1)
                swap(0, 2)
            own_terms(t)
        if 0 <= t - 1 < Z:
            stage_p(t - 1)
        if t == Z:
            swap(0, 0)
            swap(1, 0)
            local_tokens()
            for cp in state_loads:
                cp.start()
        if 0 <= t - 2 < Z:
            stage_q(t - 2)
        if t == Z + 1:
            swap(1, 1)
            swap(1, 2)
        if 0 <= t - 3 < Z:
            total = stage_z(t - 3)

    for cp in state_loads:
        cp.wait()
    for k in range(Z - 1):
        z_cp[k].wait_recv()
        total = total + rz[k].astype(f32)
    new_master, new_first, new_second = adam(total.T, state[0], state[1], state[2])
    wall[z, q] = new_master.astype(bf16)

    az, aq = {}, {}
    for j in range(1, Z):
        az[j] = send(wall.at[z, q], wall.at[z, q], az_s.at[j - 1], az_r.at[j - 1], z_at(j))

    def forward(j):
        zj = (z - j + Z) % Z
        aq[j] = send(wall.at[zj, q], wall.at[zj, q], aq_s.at[j], aq_r.at[j], q_peer)

    def product(j, i):
        zj = (z - j + Z) % Z
        qq = q if i == 0 else 1 - q
        nxt_loads[i, j].wait()
        for who in range(3):
            swaps[i, who, j].wait_recv()
        return jnp.dot(nxt[zj, qq], wall[zj, qq], preferred_element_type=f32)

    forward(0)
    for i, value in enumerate((new_master, new_first, new_second)):
        fresh[i] = value
    stores = [
        pltpu.make_async_copy(fresh.at[i], dst, fresh_sem.at[i])
        for i, dst in enumerate((nm_out, nf_out, ns_out))
    ]
    for cp in stores:
        cp.start()
    acc[...] = product(0, 0)
    for j in range(1, Z):
        az[j].wait_recv()
        forward(j)
        acc[...] += product(j, 0)
        aq[j - 1].wait_recv()
        acc[...] += product(j - 1, 1)
    aq[Z - 1].wait_recv()
    acc[...] += product(Z - 1, 1)

    last = [
        send(acc.at[pl.ds((who + 1) * rows, rows)], ro.at[who], o_s.at[who], o_r.at[who], dev)
        for who, dev in ((1, p_peer), (2, over_p(1 - c)), (0, sib))
    ]
    for cps in (core_cp, p_cp, q_cp, z_cp, az, aq, swaps):
        for cp in cps.values():
            cp.wait_send()
    for cp in stores:
        cp.wait()
    for cp in last:
        cp.wait_recv()
    out_ref[...] = (acc[pl.ds(0, rows)] + ro[0] + ro[1] + ro[2]).astype(bf16)
    for cp in last:
        cp.wait_send()


def write_out(a, b, c, d, a_out, b_out, c_out, d_out, sem):
    copies = [
        pltpu.make_async_copy(src, dst, sem.at[i])
        for i, (src, dst) in enumerate(((a, a_out), (b, b_out), (c, c_out), (d, d_out)))
    ]
    for cp in copies:
        cp.start()
    for cp in copies:
        cp.wait()


def fused(Z, tokens_in, cotangent, next_tokens, master, first_moment, second_moment):
    f32, bf16 = jnp.float32, jnp.bfloat16
    own, cols = master.shape
    count = tokens_in.shape[0]
    rows = next_tokens.shape[0]
    dma = pltpu.SemaphoreType.DMA
    block = (cols, own)
    any_spec = pl.BlockSpec(memory_space=pl.ANY)
    hbm_spec = pl.BlockSpec(memory_space=pltpu.HBM)
    scratch = [
        pltpu.VMEM((Z, PAIR * PAIR, count, PAIR * own), bf16),
        pltpu.VMEM((count, cols), bf16),
        pltpu.VMEM((Z, PAIR, 4 * rows, own), bf16),
        pltpu.VMEM((3, own, cols), f32),
        pltpu.VMEM((3, own, cols), f32),
        pltpu.VMEM((Z, PAIR, PAIR) + block, f32),
        pltpu.VMEM((Z, PAIR, PAIR) + block, bf16),
        pltpu.VMEM((Z, PAIR, PAIR) + block, bf16),
        pltpu.VMEM((Z, PAIR) + block, bf16),
        pltpu.VMEM((Z, PAIR) + block, bf16),
        pltpu.VMEM((Z,) + block, bf16),
        pltpu.VMEM((Z,) + block, bf16),
        pltpu.VMEM((Z - 1,) + block, bf16),
        pltpu.VMEM((Z - 1,) + block, bf16),
        pltpu.VMEM((Z, PAIR, own, cols), bf16),
        pltpu.VMEM((4 * rows, cols), f32),
        pltpu.VMEM((3, rows, cols), f32),
        dma((Z, PAIR * PAIR)), dma, dma((PAIR, Z)), dma((3,)), dma((3,)),
        dma((PAIR, 3, Z)), dma((PAIR, 3, Z)),
        dma((Z,)), dma((Z,)), dma((Z,)), dma((Z,)), dma((Z,)), dma((Z,)),
        dma((Z - 1,)), dma((Z - 1,)),
        dma((Z - 1,)), dma((Z - 1,)), dma((Z,)), dma((Z,)), dma((3,)), dma((3,)),
    ]
    out_shape = (
        jax.ShapeDtypeStruct(master.shape, f32),
        jax.ShapeDtypeStruct(master.shape, f32),
        jax.ShapeDtypeStruct(master.shape, f32),
        jax.ShapeDtypeStruct((rows, cols), bf16),
    )
    results = pl.pallas_call(
        functools.partial(kernel, Z, own),
        out_shape=out_shape,
        in_specs=[hbm_spec] * 6,
        out_specs=(any_spec, any_spec, any_spec, pl.BlockSpec(memory_space=pltpu.VMEM)),
        scratch_shapes=scratch,
        compiler_params=pltpu.CompilerParams(
            collective_id=0, has_side_effects=True, vmem_limit_bytes=VMEM_BYTES
        ),
    )(tokens_in, cotangent, next_tokens, master, first_moment, second_moment)
    return pl.pallas_call(
        write_out,
        out_shape=out_shape,
        in_specs=[any_spec] * 4,
        out_specs=(hbm_spec,) * 4,
        scratch_shapes=[dma((4,))],
        compiler_params=pltpu.CompilerParams(vmem_limit_bytes=VMEM_BYTES),
    )(*results)


def plain(tokens_in, cotangent, next_tokens, master, first_moment, second_moment):
    n_rep = lax.axis_size("replica")
    n_shard = lax.axis_size("shard")
    model_width = tokens_in.shape[1]
    own_rows = model_width // (n_rep * n_shard)
    blocked = lax.psum_scatter(
        lax.dot_general(
            tokens_in, cotangent, (((0,), (0,)), ((), ())), preferred_element_type=jnp.float32
        ),
        "replica",
        scatter_dimension=0,
        tiled=True,
    )
    gradient = lax.psum_scatter(blocked, "shard", scatter_dimension=0, tiled=True)
    new_master, new_first, new_second = adam(gradient, master, first_moment, second_moment)
    low_weight = new_master.astype(jnp.bfloat16)
    group_rows = lax.all_gather(low_weight, "replica", axis=0, tiled=True)
    row_count = next_tokens.shape[0]
    arranged = next_tokens.reshape(row_count, n_rep, n_shard, own_rows).transpose(0, 2, 1, 3)
    columns = arranged.reshape(row_count, model_width)
    summed = jnp.dot(
        columns,
        lax.all_gather(group_rows, "shard", axis=0, tiled=True),
        preferred_element_type=jnp.float32,
    )
    return (new_master, new_first, new_second, summed.astype(jnp.bfloat16))


def solution(mesh):
    n_rep, n_shard = mesh.shape["replica"], mesh.shape["shard"]

    def on_device(tokens_in, cotangent, next_tokens, master, first_moment, second_moment):
        own, cols = master.shape
        fits = (
            n_rep == PAIR * PAIR
            and n_shard % PAIR == 0
            and n_shard > PAIR
            and own % 128 == 0
            and cols % 128 == 0
            and next_tokens.shape[0] % 16 == 0
            and tokens_in.shape[0] % 128 == 0
        )
        args = (tokens_in, cotangent, next_tokens, master, first_moment, second_moment)
        if fits:
            return tuple(fused(n_shard // PAIR, *args))
        return plain(*args)

    spec = P(("replica", "shard"), None)
    return jax.shard_map(
        on_device, mesh=mesh, in_specs=(spec,) * 6, out_specs=(spec,) * 4, check_vma=False
    )
```

```python
import functools

import jax
import jax.numpy as jnp
from jax import lax
from jax.experimental import pallas as pl
from jax.experimental.pallas import tpu as pltpu
from jax.sharding import PartitionSpec as P

beta_one = 0.9
beta_two = 0.95
learn_rate = 0.003
decay_rate = 0.1
epsilon = 1e-08
steps_done = 10

MESH = pl.DeviceIdType.MESH
PAIR = 2
VMEM_BYTES = 62 * 2**20


def adam(gradient, master, first_moment, second_moment):
    new_first = beta_one * first_moment + (1.0 - beta_one) * gradient
    new_second = beta_two * second_moment + (1.0 - beta_two) * gradient * gradient
    first_hat = new_first / (1.0 - beta_one**steps_done)
    second_hat = new_second / (1.0 - beta_two**steps_done)
    new_master = master - learn_rate * (
        first_hat / (jnp.sqrt(second_hat) + epsilon) + decay_rate * master
    )
    return new_master, new_first, new_second


def kernel(
    Z, own,
    tok_hbm, cot_hbm, nxt_hbm, master_hbm, first_hbm, second_hbm,
    nm_out, nf_out, ns_out, out_ref,
    tok, cot, ntok, nxt, state, fresh,
    g32, gb, rc, hb, rp, jb, rq, kb, rz, wall, acc, ro,
    tok_sem, cot_sem, ntok_sem, nxt_sem, state_sem, fresh_sem,
    n_s, n_r, c_s, c_r, p_s, p_r, q_s, q_r, z_s, z_r,
    az_s, az_r, aq_s, aq_r, o_s, o_r,
):
    f32, bf16 = jnp.float32, jnp.bfloat16
    r, s = lax.axis_index("replica"), lax.axis_index("shard")
    y, c, z, x = r // PAIR, r % PAIR, s // PAIR, s % PAIR
    p, q = x * (1 - c) + y * c, y * (1 - c) + x * c
    wide = PAIR * own
    rows = nxt_hbm.shape[0]

    def at(yy, cc, zz, xx):
        return (yy * PAIR + cc, zz * PAIR + xx)

    def over_p(cc):
        return at(y * (1 - c) + (1 - y) * c, cc, z, (1 - x) * (1 - c) + x * c)

    def over_q(cc):
        return at((1 - y) * (1 - c) + y * c, cc, z, x * (1 - c) + (1 - x) * c)

    def z_at(j):
        return at(y, c, (z + j) % Z, x)

    sib, p_peer, q_peer = at(y, 1 - c, z, x), over_p(c), over_q(c)

    loads = []
    cot_load = pltpu.make_async_copy(cot_hbm, cot, cot_sem)
    cot_load.start()
    for k in range(Z):
        zc = (z + 1 + k) % Z
        row = []
        for yc in range(PAIR * PAIR):
            col = pl.multiple_of((yc * Z + zc) * wide, own)
            cp = pltpu.make_async_copy(
                tok_hbm.at[:, pl.ds(col, wide)], tok.at[k, yc], tok_sem.at[k, yc]
            )
            cp.start()
            row.append(cp)
        loads.append(row)
        if k == 0:
            barrier = pltpu.get_barrier_semaphore()
            peers = [sib, p_peer, q_peer, over_p(1 - c), over_q(1 - c)]
            peers += [z_at(j) for j in range(1, Z)]
            for d in peers:
                pl.semaphore_signal(barrier, inc=1, device_id=d, device_id_type=MESH)

    def send(src, dst, s_sem, r_sem, dev):
        cp = pltpu.make_async_remote_copy(
            src_ref=src, dst_ref=dst, send_sem=s_sem, recv_sem=r_sem,
            device_id=dev, device_id_type=MESH,
        )
        cp.start()
        return cp

    cot_load.wait()
    cot_t = cot[...].astype(f32).T.astype(bf16)
    core_cp, p_cp, q_cp, z_cp = {}, {}, {}, {}

    def term(k, h, yy, xx):
        return jnp.dot(
            cot_t, tok[k, yy * PAIR + h, :, xx * own:(xx + 1) * own],
            preferred_element_type=f32,
        )

    def place(h, yy, xx):
        return xx * (1 - h) + yy * h, yy * (1 - h) + xx * h

    def stage_core(k):
        for cp in loads[k]:
            cp.wait()
        for yy in range(PAIR):
            for xx in range(PAIR):
                gb[(k,) + place(1 - c, yy, xx)] = term(k, 1 - c, yy, xx).astype(bf16)
        if k == 0:
            pl.semaphore_wait(barrier, len(peers))
        core_cp[k] = send(gb.at[k], rc.at[k], c_s.at[k], c_r.at[k], sib)

    def own_terms(k):
        for yy in range(PAIR):
            for xx in range(PAIR):
                g32[(k,) + place(c, yy, xx)] = term(k, c, yy, xx)

    def stage_p(k):
        core_cp[k].wait_recv()
        for qq in range(PAIR):
            hb[k, qq] = (g32[k, 1 - p, qq] + rc[k, 1 - p, qq].astype(f32)).astype(bf16)
        p_cp[k] = send(hb.at[k], rp.at[k], p_s.at[k], p_r.at[k], p_peer)

    def partial(k, qq):
        return g32[k, p, qq] + rc[k, p, qq].astype(f32) + rp[k, qq].astype(f32)

    def stage_q(k):
        p_cp[k].wait_recv()
        jb[k] = partial(k, 1 - q).astype(bf16)
        q_cp[k] = send(jb.at[k], rq.at[k], q_s.at[k], q_r.at[k], q_peer)

    def stage_z(k):
        q_cp[k].wait_recv()
        total = partial(k, q) + rq[k].astype(f32)
        if k == Z - 1:
            return total
        kb[k] = total.astype(bf16)
        z_cp[k] = send(kb.at[k], rz.at[k], z_s.at[k], z_r.at[k], z_at(k + 1))
        return None

    swaps, nxt_loads, ntok_loads = {}, {}, []

    def load_tokens():
        for yy in range(PAIR):
            for h in range(PAIR):
                for zz in range(Z):
                    cp = pltpu.make_async_copy(
                        nxt_hbm.at[:, pl.ds(((yy * PAIR + h) * Z + zz) * wide, wide)],
                        ntok.at[yy, h, zz], ntok_sem.at[yy, h, zz],
                    )
                    cp.start()
                    ntok_loads.append(cp)

    def columns_for(h, pp, qq):
        yy, xx = qq * (1 - h) + pp * h, pp * (1 - h) + qq * h
        return ntok.at[yy, h, :, :, pl.ds(pl.multiple_of(xx * own, own), own)]

    def swap(i, who):
        h, pp, qq, dev = (
            (1 - c, q, p, sib), (c, 1 - p, q, p_peer), (1 - c, 1 - q, p, over_q(1 - c))
        )[who]
        qq = qq if i == 0 else 1 - qq
        swaps[i, who] = send(
            columns_for(h, pp, qq), nxt.at[qq, :, pl.ds((who + 1) * rows, rows)],
            n_s.at[i, who], n_r.at[i, who], dev,
        )

    def local_tokens(i):
        qq = q if i == 0 else 1 - q
        nxt_loads[i] = pltpu.make_async_copy(
            columns_for(c, p, qq), nxt.at[qq, :, pl.ds(0, rows)], nxt_sem.at[i]
        )
        nxt_loads[i].start()

    state_loads = [
        pltpu.make_async_copy(src, state.at[i], state_sem.at[i])
        for i, src in enumerate((master_hbm, first_hbm, second_hbm))
    ]
    total = None
    for t in range(Z + 4):
        if t < Z:
            stage_core(t)
            own_terms(t)
        if 0 <= t - 1 < Z:
            stage_p(t - 1)
        if t == 1:
            load_tokens()
            for cp in state_loads:
                cp.start()
        if t == Z:
            for cp in ntok_loads:
                cp.wait()
            for i in range(PAIR):
                local_tokens(i)
                swap(i, 0)
        if 0 <= t - 3 < Z:
            stage_q(t - 3)
        if t == Z + 2:
            for i in range(PAIR):
                swap(i, 1)
                swap(i, 2)
        if 0 <= t - 4 < Z:
            total = stage_z(t - 4)

    for cp in state_loads:
        cp.wait()
    for k in range(Z - 1):
        z_cp[k].wait_recv()
        total = total + rz[k].astype(f32)
    new_master, new_first, new_second = adam(total.T, state[0], state[1], state[2])
    wall[z, q] = new_master.astype(bf16)

    az, aq = {}, {}
    for j in range(1, Z):
        az[j] = send(wall.at[z, q], wall.at[z, q], az_s.at[j - 1], az_r.at[j - 1], z_at(j))

    def forward(j):
        zj = (z - j + Z) % Z
        aq[j] = send(wall.at[zj, q], wall.at[zj, q], aq_s.at[j], aq_r.at[j], q_peer)

    def product(j, i):
        zj = (z - j + Z) % Z
        qq = q if i == 0 else 1 - q
        if j == 0:
            nxt_loads[i].wait()
            for who in range(3):
                swaps[i, who].wait_recv()
        return jnp.dot(nxt[qq, zj], wall[zj, qq], preferred_element_type=f32)

    forward(0)
    for i, value in enumerate((new_master, new_first, new_second)):
        fresh[i] = value
    stores = [
        pltpu.make_async_copy(fresh.at[i], dst, fresh_sem.at[i])
        for i, dst in enumerate((nm_out, nf_out, ns_out))
    ]
    for cp in stores:
        cp.start()
    acc[...] = product(0, 0)
    for j in range(1, Z):
        az[j].wait_recv()
        forward(j)
        acc[...] += product(j, 0)
        aq[j - 1].wait_recv()
        acc[...] += product(j - 1, 1)
    aq[Z - 1].wait_recv()
    acc[...] += product(Z - 1, 1)

    last = [
        send(acc.at[pl.ds((who + 1) * rows, rows)], ro.at[who], o_s.at[who], o_r.at[who], dev)
        for who, dev in ((1, p_peer), (2, over_p(1 - c)), (0, sib))
    ]
    for cps in (core_cp, p_cp, q_cp, z_cp, az, aq, swaps):
        for cp in cps.values():
            cp.wait_send()
    for cp in stores:
        cp.wait()
    for cp in last:
        cp.wait_recv()
    out_ref[...] = (acc[pl.ds(0, rows)] + ro[0] + ro[1] + ro[2]).astype(bf16)
    for cp in last:
        cp.wait_send()


def write_out(a, b, c, d, a_out, b_out, c_out, d_out):
    a_out[...] = a[...]
    b_out[...] = b[...]
    c_out[...] = c[...]
    d_out[...] = d[...]


def fused(Z, tokens_in, cotangent, next_tokens, master, first_moment, second_moment):
    f32, bf16 = jnp.float32, jnp.bfloat16
    own, cols = master.shape
    count = tokens_in.shape[0]
    rows = next_tokens.shape[0]
    dma = pltpu.SemaphoreType.DMA
    block = (cols, own)
    any_spec = pl.BlockSpec(memory_space=pl.ANY)
    hbm_spec = pl.BlockSpec(memory_space=pltpu.HBM)
    scratch = [
        pltpu.VMEM((Z, PAIR * PAIR, count, PAIR * own), bf16),
        pltpu.VMEM((count, cols), bf16),
        pltpu.VMEM((PAIR, PAIR, Z, rows, PAIR * own), bf16),
        pltpu.VMEM((PAIR, Z, 4 * rows, own), bf16),
        pltpu.VMEM((3, own, cols), f32),
        pltpu.VMEM((3, own, cols), f32),
        pltpu.VMEM((Z, PAIR, PAIR) + block, f32),
        pltpu.VMEM((Z, PAIR, PAIR) + block, bf16),
        pltpu.VMEM((Z, PAIR, PAIR) + block, bf16),
        pltpu.VMEM((Z, PAIR) + block, bf16),
        pltpu.VMEM((Z, PAIR) + block, bf16),
        pltpu.VMEM((Z,) + block, bf16),
        pltpu.VMEM((Z,) + block, bf16),
        pltpu.VMEM((Z - 1,) + block, bf16),
        pltpu.VMEM((Z - 1,) + block, bf16),
        pltpu.VMEM((Z, PAIR, own, cols), bf16),
        pltpu.VMEM((4 * rows, cols), f32),
        pltpu.VMEM((3, rows, cols), f32),
        dma((Z, PAIR * PAIR)), dma, dma((PAIR, PAIR, Z)), dma((PAIR,)), dma((3,)), dma((3,)),
        dma((PAIR, 3)), dma((PAIR, 3)),
        dma((Z,)), dma((Z,)), dma((Z,)), dma((Z,)), dma((Z,)), dma((Z,)),
        dma((Z - 1,)), dma((Z - 1,)),
        dma((Z - 1,)), dma((Z - 1,)), dma((Z,)), dma((Z,)), dma((3,)), dma((3,)),
    ]
    out_shape = (
        jax.ShapeDtypeStruct(master.shape, f32),
        jax.ShapeDtypeStruct(master.shape, f32),
        jax.ShapeDtypeStruct(master.shape, f32),
        jax.ShapeDtypeStruct((rows, cols), bf16),
    )
    results = pl.pallas_call(
        functools.partial(kernel, Z, own),
        out_shape=out_shape,
        in_specs=[hbm_spec] * 6,
        out_specs=(any_spec, any_spec, any_spec, pl.BlockSpec(memory_space=pltpu.VMEM)),
        scratch_shapes=scratch,
        compiler_params=pltpu.CompilerParams(
            collective_id=0, has_side_effects=True, vmem_limit_bytes=VMEM_BYTES
        ),
    )(tokens_in, cotangent, next_tokens, master, first_moment, second_moment)
    vmem_spec = pl.BlockSpec(memory_space=pltpu.VMEM)
    return pl.pallas_call(
        write_out,
        out_shape=out_shape,
        in_specs=[vmem_spec] * 4,
        out_specs=(vmem_spec,) * 4,
        compiler_params=pltpu.CompilerParams(vmem_limit_bytes=VMEM_BYTES),
    )(*results)


def plain(tokens_in, cotangent, next_tokens, master, first_moment, second_moment):
    n_rep = lax.axis_size("replica")
    n_shard = lax.axis_size("shard")
    model_width = tokens_in.shape[1]
    own_rows = model_width // (n_rep * n_shard)
    blocked = lax.psum_scatter(
        lax.dot_general(
            tokens_in, cotangent, (((0,), (0,)), ((), ())), preferred_element_type=jnp.float32
        ),
        "replica",
        scatter_dimension=0,
        tiled=True,
    )
    gradient = lax.psum_scatter(blocked, "shard", scatter_dimension=0, tiled=True)
    new_master, new_first, new_second = adam(gradient, master, first_moment, second_moment)
    low_weight = new_master.astype(jnp.bfloat16)
    group_rows = lax.all_gather(low_weight, "replica", axis=0, tiled=True)
    row_count = next_tokens.shape[0]
    arranged = next_tokens.reshape(row_count, n_rep, n_shard, own_rows).transpose(0, 2, 1, 3)
    columns = arranged.reshape(row_count, model_width)
    summed = jnp.dot(
        columns,
        lax.all_gather(group_rows, "shard", axis=0, tiled=True),
        preferred_element_type=jnp.float32,
    )
    return (new_master, new_first, new_second, summed.astype(jnp.bfloat16))


def solution(mesh):
    n_rep, n_shard = mesh.shape["replica"], mesh.shape["shard"]

    def on_device(tokens_in, cotangent, next_tokens, master, first_moment, second_moment):
        own, cols = master.shape
        fits = (
            n_rep == PAIR * PAIR
            and n_shard % PAIR == 0
            and n_shard > PAIR
            and own % 128 == 0
            and cols % 128 == 0
            and next_tokens.shape[0] % 16 == 0
            and tokens_in.shape[0] % 128 == 0
        )
        args = (tokens_in, cotangent, next_tokens, master, first_moment, second_moment)
        if fits:
            return tuple(fused(n_shard // PAIR, *args))
        return plain(*args)

    spec = P(("replica", "shard"), None)
    return jax.shard_map(
        on_device, mesh=mesh, in_specs=(spec,) * 6, out_specs=(spec,) * 4, check_vma=False
    )
```

```python
import functools

import jax
import jax.numpy as jnp
from jax import lax
from jax.experimental import pallas as pl
from jax.experimental.pallas import tpu as pltpu
from jax.sharding import PartitionSpec as P

beta_one = 0.9
beta_two = 0.95
learn_rate = 0.003
decay_rate = 0.1
epsilon = 1e-08
steps_done = 10

MESH = pl.DeviceIdType.MESH
PAIR = 2
VMEM_BYTES = 62 * 2**20


def adam(gradient, master, first_moment, second_moment):
    new_first = beta_one * first_moment + (1.0 - beta_one) * gradient
    new_second = beta_two * second_moment + (1.0 - beta_two) * gradient * gradient
    first_hat = new_first / (1.0 - beta_one**steps_done)
    second_hat = new_second / (1.0 - beta_two**steps_done)
    new_master = master - learn_rate * (
        first_hat / (jnp.sqrt(second_hat) + epsilon) + decay_rate * master
    )
    return new_master, new_first, new_second


def kernel(
    Z, own,
    tok_hbm, cot_hbm, nxt_hbm, master_hbm, first_hbm, second_hbm,
    nm_out, nf_out, ns_out, out_ref,
    tok, cot, ntok, nxt, state,
    g32, gb, rc, hb, rp, jb, rq, kb, rz, wall, acc, ro,
    tok_sem, cot_sem, ntok_sem, nxt_sem, state_sem,
    n_s, n_r, c_s, c_r, p_s, p_r, q_s, q_r, z_s, z_r,
    az_s, az_r, aq_s, aq_r, o_s, o_r,
):
    f32, bf16 = jnp.float32, jnp.bfloat16
    r, s = lax.axis_index("replica"), lax.axis_index("shard")
    y, c, z, x = r // PAIR, r % PAIR, s // PAIR, s % PAIR
    p, q = x * (1 - c) + y * c, y * (1 - c) + x * c
    wide = PAIR * own
    rows = nxt_hbm.shape[0]

    def at(yy, cc, zz, xx):
        return (yy * PAIR + cc, zz * PAIR + xx)

    def over_p(cc):
        return at(y * (1 - c) + (1 - y) * c, cc, z, (1 - x) * (1 - c) + x * c)

    def over_q(cc):
        return at((1 - y) * (1 - c) + y * c, cc, z, x * (1 - c) + (1 - x) * c)

    def z_at(j):
        return at(y, c, (z + j) % Z, x)

    sib, p_peer, q_peer = at(y, 1 - c, z, x), over_p(c), over_q(c)

    barrier = pltpu.get_barrier_semaphore()
    peers = [sib, p_peer, q_peer, over_p(1 - c), over_q(1 - c)]
    peers += [z_at(j) for j in range(1, Z)]
    for d in peers:
        pl.semaphore_signal(barrier, inc=1, device_id=d, device_id_type=MESH)

    loads = []
    cot_load = pltpu.make_async_copy(cot_hbm, cot, cot_sem)
    cot_load.start()
    for k in range(Z):
        zc = (z + 1 + k) % Z
        row = []
        for yc in range(PAIR * PAIR):
            col = pl.multiple_of((yc * Z + zc) * wide, own)
            cp = pltpu.make_async_copy(
                tok_hbm.at[:, pl.ds(col, wide)], tok.at[k, yc], tok_sem.at[k, yc]
            )
            cp.start()
            row.append(cp)
        loads.append(row)

    def send(src, dst, s_sem, r_sem, dev):
        cp = pltpu.make_async_remote_copy(
            src_ref=src, dst_ref=dst, send_sem=s_sem, recv_sem=r_sem,
            device_id=dev, device_id_type=MESH,
        )
        cp.start()
        return cp

    cot_load.wait()
    cot_t = cot[...].astype(f32).T.astype(bf16)
    core_cp, p_cp, q_cp, z_cp = {}, {}, {}, {}

    def term(k, h, yy, xx):
        return jnp.dot(
            cot_t, tok[k, yy * PAIR + h, :, xx * own:(xx + 1) * own],
            preferred_element_type=f32,
        )

    def place(h, yy, xx):
        return xx * (1 - h) + yy * h, yy * (1 - h) + xx * h

    def stage_core(k):
        for cp in loads[k]:
            cp.wait()
        for yy in range(PAIR):
            for xx in range(PAIR):
                gb[(k,) + place(1 - c, yy, xx)] = term(k, 1 - c, yy, xx).astype(bf16)
        if k == 0:
            pl.semaphore_wait(barrier, len(peers))
        core_cp[k] = send(gb.at[k], rc.at[k], c_s.at[k], c_r.at[k], sib)

    def own_terms(k):
        for yy in range(PAIR):
            for xx in range(PAIR):
                g32[(k,) + place(c, yy, xx)] = term(k, c, yy, xx)

    def stage_p(k):
        core_cp[k].wait_recv()
        for qq in range(PAIR):
            hb[k, qq] = (g32[k, 1 - p, qq] + rc[k, 1 - p, qq].astype(f32)).astype(bf16)
        p_cp[k] = send(hb.at[k], rp.at[k], p_s.at[k], p_r.at[k], p_peer)

    def partial(k, qq):
        return g32[k, p, qq] + rc[k, p, qq].astype(f32) + rp[k, qq].astype(f32)

    def stage_q(k):
        p_cp[k].wait_recv()
        jb[k] = partial(k, 1 - q).astype(bf16)
        q_cp[k] = send(jb.at[k], rq.at[k], q_s.at[k], q_r.at[k], q_peer)

    def stage_z(k):
        q_cp[k].wait_recv()
        total = partial(k, q) + rq[k].astype(f32)
        if k == Z - 1:
            return total
        kb[k] = total.astype(bf16)
        z_cp[k] = send(kb.at[k], rz.at[k], z_s.at[k], z_r.at[k], z_at(k + 1))
        return None

    swaps, nxt_loads, ntok_loads = {}, {}, []

    def load_tokens():
        for yy in range(PAIR):
            for h in range(PAIR):
                for zz in range(Z):
                    cp = pltpu.make_async_copy(
                        nxt_hbm.at[:, pl.ds(((yy * PAIR + h) * Z + zz) * wide, wide)],
                        ntok.at[yy, h, zz], ntok_sem.at[yy, h, zz],
                    )
                    cp.start()
                    ntok_loads.append(cp)

    def columns_for(h, pp, qq):
        yy, xx = qq * (1 - h) + pp * h, pp * (1 - h) + qq * h
        return ntok.at[yy, h, :, :, pl.ds(pl.multiple_of(xx * own, own), own)]

    def swap(i, who):
        h, pp, qq, dev = (
            (1 - c, q, p, sib), (c, 1 - p, q, p_peer), (1 - c, 1 - q, p, over_q(1 - c))
        )[who]
        qq = qq if i == 0 else 1 - qq
        swaps[i, who] = send(
            columns_for(h, pp, qq), nxt.at[qq, :, pl.ds((who + 1) * rows, rows)],
            n_s.at[i, who], n_r.at[i, who], dev,
        )

    def local_tokens(i):
        qq = q if i == 0 else 1 - q
        nxt_loads[i] = pltpu.make_async_copy(
            columns_for(c, p, qq), nxt.at[qq, :, pl.ds(0, rows)], nxt_sem.at[i]
        )
        nxt_loads[i].start()

    state_loads = [
        pltpu.make_async_copy(src, state.at[i], state_sem.at[i])
        for i, src in enumerate((master_hbm, first_hbm, second_hbm))
    ]
    total = None
    for t in range(Z + 4):
        if t < Z:
            stage_core(t)
            own_terms(t)
        if 0 <= t - 1 < Z:
            stage_p(t - 1)
        if t == 1:
            load_tokens()
            for cp in state_loads:
                cp.start()
        if t == Z:
            for cp in ntok_loads:
                cp.wait()
            for i in range(PAIR):
                local_tokens(i)
                swap(i, 0)
        if 0 <= t - 3 < Z:
            stage_q(t - 3)
        if t == Z + 2:
            for i in range(PAIR):
                swap(i, 1)
                swap(i, 2)
        if 0 <= t - 4 < Z:
            total = stage_z(t - 4)

    for cp in state_loads:
        cp.wait()
    for k in range(Z - 1):
        z_cp[k].wait_recv()

    az, aq, stores = {}, {}, []
    half = own // 2

    def piece(zz, hh):
        return wall.at[zz, q, pl.ds(hh * half, half)]

    def forward(j, hh):
        part = piece((z - j + Z) % Z, hh)
        aq[j, hh] = send(part, part, aq_s.at[j, hh], aq_r.at[j, hh], q_peer)

    for hh in range(2):
        part = pl.ds(hh * half, half)
        gradient = total[:, hh * half:(hh + 1) * half]
        for k in range(Z - 1):
            gradient = gradient + rz[k, :, part].astype(f32)
        new_master, new_first, new_second = adam(
            gradient.T, state[0, part], state[1, part], state[2, part]
        )
        wall[z, q, part] = new_master.astype(bf16)
        for j in range(1, Z):
            az[j, hh] = send(
                piece(z, hh), piece(z, hh), az_s.at[j - 1, hh], az_r.at[j - 1, hh], z_at(j)
            )
        forward(0, hh)
        nm_out[part] = new_master
        nf_out[part] = new_first
        ns_out[part] = new_second

    def product(j, i, first, count):
        zj = (z - j + Z) % Z
        qq = q if i == 0 else 1 - q
        return jnp.dot(
            nxt[qq, zj, pl.ds(first, count)], wall[zj, qq], preferred_element_type=f32
        )

    def tokens_here(i):
        nxt_loads[i].wait()
        for who in range(3):
            swaps[i, who].wait_recv()

    tokens_here(0)
    acc[...] = product(0, 0, 0, 4 * rows)
    for j in range(1, Z):
        for hh in range(2):
            az[j, hh].wait_recv()
            forward(j, hh)
        acc[...] += product(j, 0, 0, 4 * rows)
        if j == 1:
            tokens_here(1)
        for hh in range(2):
            aq[j - 1, hh].wait_recv()
        acc[...] += product(j - 1, 1, 0, 4 * rows)
    for hh in range(2):
        aq[Z - 1, hh].wait_recv()

    far, near = pl.ds(2 * rows, 2 * rows), pl.ds(0, 2 * rows)
    acc[far] += product(Z - 1, 1, 2 * rows, 2 * rows)

    def part_to(who, dev):
        return send(
            acc.at[pl.ds((who + 1) * rows, rows)], ro.at[who], o_s.at[who], o_r.at[who], dev
        )

    last = [part_to(1, p_peer), part_to(2, over_p(1 - c))]
    acc[near] += product(Z - 1, 1, 0, 2 * rows)
    last.append(part_to(0, sib))
    for cps in (core_cp, p_cp, q_cp, z_cp, az, aq, swaps):
        for cp in cps.values():
            cp.wait_send()
    for cp in last:
        cp.wait_recv()
    out_ref[...] = (acc[pl.ds(0, rows)] + ro[0] + ro[1] + ro[2]).astype(bf16)
    for cp in last:
        cp.wait_send()


def write_out(a, b, c, d, a_out, b_out, c_out, d_out):
    a_out[...] = a[...]
    b_out[...] = b[...]
    c_out[...] = c[...]
    d_out[...] = d[...]


def fused(Z, tokens_in, cotangent, next_tokens, master, first_moment, second_moment):
    f32, bf16 = jnp.float32, jnp.bfloat16
    own, cols = master.shape
    count = tokens_in.shape[0]
    rows = next_tokens.shape[0]
    dma = pltpu.SemaphoreType.DMA
    block = (cols, own)
    vmem_spec = pl.BlockSpec(memory_space=pltpu.VMEM)
    hbm_spec = pl.BlockSpec(memory_space=pltpu.HBM)
    scratch = [
        pltpu.VMEM((Z, PAIR * PAIR, count, PAIR * own), bf16),
        pltpu.VMEM((count, cols), bf16),
        pltpu.VMEM((PAIR, PAIR, Z, rows, PAIR * own), bf16),
        pltpu.VMEM((PAIR, Z, 4 * rows, own), bf16),
        pltpu.VMEM((3, own, cols), f32),
        pltpu.VMEM((Z, PAIR, PAIR) + block, f32),
        pltpu.VMEM((Z, PAIR, PAIR) + block, bf16),
        pltpu.VMEM((Z, PAIR, PAIR) + block, bf16),
        pltpu.VMEM((Z, PAIR) + block, bf16),
        pltpu.VMEM((Z, PAIR) + block, bf16),
        pltpu.VMEM((Z,) + block, bf16),
        pltpu.VMEM((Z,) + block, bf16),
        pltpu.VMEM((Z - 1,) + block, bf16),
        pltpu.VMEM((Z - 1,) + block, bf16),
        pltpu.VMEM((Z, PAIR, own, cols), bf16),
        pltpu.VMEM((4 * rows, cols), f32),
        pltpu.VMEM((3, rows, cols), f32),
        dma((Z, PAIR * PAIR)), dma, dma((PAIR, PAIR, Z)), dma((PAIR,)), dma((3,)),
        dma((PAIR, 3)), dma((PAIR, 3)),
        dma((Z,)), dma((Z,)), dma((Z,)), dma((Z,)), dma((Z,)), dma((Z,)),
        dma((Z - 1,)), dma((Z - 1,)),
        dma((Z - 1, 2)), dma((Z - 1, 2)), dma((Z, 2)), dma((Z, 2)), dma((3,)), dma((3,)),
    ]
    out_shape = (
        jax.ShapeDtypeStruct(master.shape, f32),
        jax.ShapeDtypeStruct(master.shape, f32),
        jax.ShapeDtypeStruct(master.shape, f32),
        jax.ShapeDtypeStruct((rows, cols), bf16),
    )
    results = pl.pallas_call(
        functools.partial(kernel, Z, own),
        out_shape=tuple(pltpu.VMEM(a.shape, a.dtype) for a in out_shape),
        in_specs=[hbm_spec] * 6,
        out_specs=(vmem_spec,) * 4,
        scratch_shapes=scratch,
        compiler_params=pltpu.CompilerParams(
            collective_id=0, has_side_effects=True, vmem_limit_bytes=VMEM_BYTES
        ),
    )(tokens_in, cotangent, next_tokens, master, first_moment, second_moment)
    return pl.pallas_call(
        write_out,
        out_shape=out_shape,
        in_specs=[vmem_spec] * 4,
        out_specs=(vmem_spec,) * 4,
        compiler_params=pltpu.CompilerParams(vmem_limit_bytes=VMEM_BYTES // 8),
    )(*results)


def plain(tokens_in, cotangent, next_tokens, master, first_moment, second_moment):
    n_rep = lax.axis_size("replica")
    n_shard = lax.axis_size("shard")
    model_width = tokens_in.shape[1]
    own_rows = model_width // (n_rep * n_shard)
    blocked = lax.psum_scatter(
        lax.dot_general(
            tokens_in, cotangent, (((0,), (0,)), ((), ())), preferred_element_type=jnp.float32
        ),
        "replica",
        scatter_dimension=0,
        tiled=True,
    )
    gradient = lax.psum_scatter(blocked, "shard", scatter_dimension=0, tiled=True)
    new_master, new_first, new_second = adam(gradient, master, first_moment, second_moment)
    low_weight = new_master.astype(jnp.bfloat16)
    group_rows = lax.all_gather(low_weight, "replica", axis=0, tiled=True)
    row_count = next_tokens.shape[0]
    arranged = next_tokens.reshape(row_count, n_rep, n_shard, own_rows).transpose(0, 2, 1, 3)
    columns = arranged.reshape(row_count, model_width)
    summed = jnp.dot(
        columns,
        lax.all_gather(group_rows, "shard", axis=0, tiled=True),
        preferred_element_type=jnp.float32,
    )
    return (new_master, new_first, new_second, summed.astype(jnp.bfloat16))


def solution(mesh):
    n_rep, n_shard = mesh.shape["replica"], mesh.shape["shard"]

    def on_device(tokens_in, cotangent, next_tokens, master, first_moment, second_moment):
        own, cols = master.shape
        fits = (
            n_rep == PAIR * PAIR
            and n_shard % PAIR == 0
            and n_shard > PAIR
            and own % 256 == 0
            and cols % 128 == 0
            and next_tokens.shape[0] % 16 == 0
            and tokens_in.shape[0] % 128 == 0
        )
        args = (tokens_in, cotangent, next_tokens, master, first_moment, second_moment)
        if fits:
            return tuple(fused(n_shard // PAIR, *args))
        return plain(*args)

    spec = P(("replica", "shard"), None)
    return jax.shard_map(
        on_device, mesh=mesh, in_specs=(spec,) * 6, out_specs=(spec,) * 4, check_vma=False
    )
```

```python
import functools

import jax
import jax.numpy as jnp
from jax import lax
from jax.experimental import pallas as pl
from jax.experimental.pallas import tpu as pltpu
from jax.sharding import PartitionSpec as P

beta_one = 0.9
beta_two = 0.95
learn_rate = 0.003
decay_rate = 0.1
epsilon = 1e-08
steps_done = 10

MESH = pl.DeviceIdType.MESH
PAIR = 2
VMEM_BYTES = 62 * 2**20


def adam(gradient, master, first_moment, second_moment):
    new_first = beta_one * first_moment + (1.0 - beta_one) * gradient
    new_second = beta_two * second_moment + (1.0 - beta_two) * gradient * gradient
    first_hat = new_first / (1.0 - beta_one**steps_done)
    second_hat = new_second / (1.0 - beta_two**steps_done)
    new_master = master - learn_rate * (
        first_hat / (jnp.sqrt(second_hat) + epsilon) + decay_rate * master
    )
    return new_master, new_first, new_second


def kernel(
    Z, own,
    tok_hbm, cot_hbm, nxt_hbm, master_hbm, first_hbm, second_hbm,
    nm_out, nf_out, ns_out, out_ref,
    tok, cot, ntok, nxt, state,
    g32, gb, rc, hb, rp, jb, rq, kb, rz, wall, acc, ro,
    tok_sem, cot_sem, ntok_sem, nxt_sem, state_sem,
    n_s, n_r, c_s, c_r, p_s, p_r, q_s, q_r, z_s, z_r,
    az_s, az_r, aq_s, aq_r, o_s, o_r,
):
    f32, bf16 = jnp.float32, jnp.bfloat16
    r, s = lax.axis_index("replica"), lax.axis_index("shard")
    y, c, z, x = r // PAIR, r % PAIR, s // PAIR, s % PAIR
    p, q = x * (1 - c) + y * c, y * (1 - c) + x * c
    wide = PAIR * own
    rows = nxt_hbm.shape[0]

    def at(yy, cc, zz, xx):
        return (yy * PAIR + cc, zz * PAIR + xx)

    def over_p(cc):
        return at(y * (1 - c) + (1 - y) * c, cc, z, (1 - x) * (1 - c) + x * c)

    def over_q(cc):
        return at((1 - y) * (1 - c) + y * c, cc, z, x * (1 - c) + (1 - x) * c)

    def z_of(d):
        zz, bit = z, 1
        while bit < Z:
            if d & bit:
                zz = zz + bit - 2 * bit * ((zz // bit) % 2)
            bit *= 2
        return zz

    def z_at(d):
        return at(y, c, z_of(d), x)

    sib, p_peer, q_peer = at(y, 1 - c, z, x), over_p(c), over_q(c)

    barrier = pltpu.get_barrier_semaphore()
    peers = [sib, p_peer, q_peer, over_p(1 - c), over_q(1 - c)]
    peers += [z_at(j) for j in range(1, Z)]
    for d in peers:
        pl.semaphore_signal(barrier, inc=1, device_id=d, device_id_type=MESH)

    loads, ntok_loads = [], []
    cot_load = pltpu.make_async_copy(cot_hbm, cot, cot_sem)
    cot_load.start()
    for k in range(Z):
        zc = z_of(Z - 1 - k)
        row = []
        for yc in range(PAIR * PAIR):
            col = pl.multiple_of((yc * Z + zc) * wide, own)
            cp = pltpu.make_async_copy(
                tok_hbm.at[:, pl.ds(col, wide)], tok.at[k, yc], tok_sem.at[k, yc]
            )
            cp.start()
            row.append(cp)
        loads.append(row)
        if k == 0:
            for yy in range(PAIR):
                for h in range(PAIR):
                    for zz in range(Z):
                        cp = pltpu.make_async_copy(
                            nxt_hbm.at[:, pl.ds(((yy * PAIR + h) * Z + zz) * wide, wide)],
                            ntok.at[yy, h, zz], ntok_sem.at[yy, h, zz],
                        )
                        cp.start()
                        ntok_loads.append(cp)

    def send(src, dst, s_sem, r_sem, dev):
        cp = pltpu.make_async_remote_copy(
            src_ref=src, dst_ref=dst, send_sem=s_sem, recv_sem=r_sem,
            device_id=dev, device_id_type=MESH,
        )
        cp.start()
        return cp

    cot_load.wait()
    cot_t = cot[...].astype(f32).T.astype(bf16)
    core_cp, p_cp, q_cp, z_cp = {}, {}, {}, {}

    def term(k, h, yy, xx):
        return jnp.dot(
            cot_t, tok[k, yy * PAIR + h, :, xx * own:(xx + 1) * own],
            preferred_element_type=f32,
        )

    def place(h, yy, xx):
        return xx * (1 - h) + yy * h, yy * (1 - h) + xx * h

    def stage_core(k):
        for cp in loads[k]:
            cp.wait()
        for yy in range(PAIR):
            for xx in range(PAIR):
                gb[(k,) + place(1 - c, yy, xx)] = term(k, 1 - c, yy, xx).astype(bf16)
        if k == 0:
            pl.semaphore_wait(barrier, len(peers))
        core_cp[k] = send(gb.at[k], rc.at[k], c_s.at[k], c_r.at[k], sib)

    def own_terms(k):
        for yy in range(PAIR):
            for xx in range(PAIR):
                g32[(k,) + place(c, yy, xx)] = term(k, c, yy, xx)

    def stage_p(k):
        core_cp[k].wait_recv()
        for qq in range(PAIR):
            hb[k, qq] = (g32[k, 1 - p, qq] + rc[k, 1 - p, qq].astype(f32)).astype(bf16)
        p_cp[k] = send(hb.at[k], rp.at[k], p_s.at[k], p_r.at[k], p_peer)

    def partial(k, qq):
        return g32[k, p, qq] + rc[k, p, qq].astype(f32) + rp[k, qq].astype(f32)

    def stage_q(k):
        p_cp[k].wait_recv()
        jb[k] = partial(k, 1 - q).astype(bf16)
        q_cp[k] = send(jb.at[k], rq.at[k], q_s.at[k], q_r.at[k], q_peer)

    def stage_z(k):
        q_cp[k].wait_recv()
        total = partial(k, q) + rq[k].astype(f32)
        if k == Z - 1:
            return total
        kb[k] = total.astype(bf16)
        z_cp[k] = send(kb.at[k], rz.at[k], z_s.at[k], z_r.at[k], z_at(Z - 1 - k))
        return None

    swaps, nxt_loads = {}, {}

    def columns_for(h, pp, qq):
        yy, xx = qq * (1 - h) + pp * h, pp * (1 - h) + qq * h
        return ntok.at[yy, h, :, :, pl.ds(pl.multiple_of(xx * own, own), own)]

    def swap(i, who):
        h, pp, qq, dev = (
            (1 - c, q, p, sib), (c, 1 - p, q, p_peer), (1 - c, 1 - q, p, over_q(1 - c))
        )[who]
        qq = qq if i == 0 else 1 - qq
        swaps[i, who] = send(
            columns_for(h, pp, qq), nxt.at[qq, :, pl.ds((who + 1) * rows, rows)],
            n_s.at[i, who], n_r.at[i, who], dev,
        )

    def local_tokens(i):
        qq = q if i == 0 else 1 - q
        nxt_loads[i] = pltpu.make_async_copy(
            columns_for(c, p, qq), nxt.at[qq, :, pl.ds(0, rows)], nxt_sem.at[i]
        )
        nxt_loads[i].start()

    state_loads = [
        pltpu.make_async_copy(src, state.at[i], state_sem.at[i])
        for i, src in enumerate((master_hbm, first_hbm, second_hbm))
    ]
    total = None
    for t in range(Z + 4):
        if t < Z:
            stage_core(t)
            if t == 0:
                for cp in ntok_loads:
                    cp.wait()
                swap(0, 1)
                swap(0, 2)
            own_terms(t)
        if 0 <= t - 1 < Z:
            stage_p(t - 1)
        if t == 1:
            for cp in state_loads:
                cp.start()
        if t == Z:
            for i in range(PAIR):
                local_tokens(i)
                swap(i, 0)
        if 0 <= t - 3 < Z:
            stage_q(t - 3)
        if t == Z + 2:
            swap(1, 1)
            swap(1, 2)
        if 0 <= t - 4 < Z:
            total = stage_z(t - 4)

    for cp in state_loads:
        cp.wait()
    for k in range(Z - 1):
        z_cp[k].wait_recv()

    az, aq, stores = {}, {}, []
    half = own // 2

    def piece(zz, hh):
        return wall.at[zz, q, pl.ds(hh * half, half)]

    def forward(j, hh):
        part = piece(z_of(j), hh)
        aq[j, hh] = send(part, part, aq_s.at[j, hh], aq_r.at[j, hh], q_peer)

    for hh in range(2):
        part = pl.ds(hh * half, half)
        gradient = total[:, hh * half:(hh + 1) * half]
        for k in range(Z - 1):
            gradient = gradient + rz[k, :, part].astype(f32)
        new_master, new_first, new_second = adam(
            gradient.T, state[0, part], state[1, part], state[2, part]
        )
        wall[z, q, part] = new_master.astype(bf16)
        for j in range(Z - 1, 0, -1):
            az[j, hh] = send(
                piece(z, hh), piece(z, hh), az_s.at[j - 1, hh], az_r.at[j - 1, hh], z_at(j)
            )
        forward(0, hh)
        nm_out[part] = new_master
        nf_out[part] = new_first
        ns_out[part] = new_second

    def product(j, i, first, count):
        zj = z_of(j)
        qq = q if i == 0 else 1 - q
        return jnp.dot(
            nxt[qq, zj, pl.ds(first, count)], wall[zj, qq], preferred_element_type=f32
        )

    def tokens_here(i):
        nxt_loads[i].wait()
        for who in range(3):
            swaps[i, who].wait_recv()

    order = [0] + list(range(Z - 1, 0, -1))

    def second(n):
        for hh in range(2):
            aq[order[n], hh].wait_recv()
        return product(order[n], 1, 0, 4 * rows)

    for n in range(1, Z):
        for hh in range(2):
            az[order[n], hh].wait_recv()
            forward(order[n], hh)
        if n == 1:
            tokens_here(0)
            acc[...] = product(0, 0, 0, 4 * rows)
        if n == 2:
            tokens_here(1)
        acc[...] += product(order[n], 0, 0, 4 * rows)
        if n >= 2:
            acc[...] += second(n - 2)
    acc[...] += second(Z - 2)
    end = order[Z - 1]
    for hh in range(2):
        aq[end, hh].wait_recv()

    far, near = pl.ds(2 * rows, 2 * rows), pl.ds(0, 2 * rows)
    acc[far] += product(end, 1, 2 * rows, 2 * rows)

    def part_to(who, dev):
        return send(
            acc.at[pl.ds((who + 1) * rows, rows)], ro.at[who], o_s.at[who], o_r.at[who], dev
        )

    last = [part_to(1, p_peer), part_to(2, over_p(1 - c))]
    acc[near] += product(end, 1, 0, 2 * rows)
    last.append(part_to(0, sib))
    for cps in (core_cp, p_cp, q_cp, z_cp, az, aq, swaps):
        for cp in cps.values():
            cp.wait_send()
    for cp in last:
        cp.wait_recv()
    out_ref[...] = (acc[pl.ds(0, rows)] + ro[0] + ro[1] + ro[2]).astype(bf16)
    for cp in last:
        cp.wait_send()


def write_out(a, b, c, d, a_out, b_out, c_out, d_out):
    a_out[...] = a[...]
    b_out[...] = b[...]
    c_out[...] = c[...]
    d_out[...] = d[...]


def fused(Z, tokens_in, cotangent, next_tokens, master, first_moment, second_moment):
    f32, bf16 = jnp.float32, jnp.bfloat16
    own, cols = master.shape
    count = tokens_in.shape[0]
    rows = next_tokens.shape[0]
    dma = pltpu.SemaphoreType.DMA
    block = (cols, own)
    vmem_spec = pl.BlockSpec(memory_space=pltpu.VMEM)
    hbm_spec = pl.BlockSpec(memory_space=pltpu.HBM)
    scratch = [
        pltpu.VMEM((Z, PAIR * PAIR, count, PAIR * own), bf16),
        pltpu.VMEM((count, cols), bf16),
        pltpu.VMEM((PAIR, PAIR, Z, rows, PAIR * own), bf16),
        pltpu.VMEM((PAIR, Z, 4 * rows, own), bf16),
        pltpu.VMEM((3, own, cols), f32),
        pltpu.VMEM((Z, PAIR, PAIR) + block, f32),
        pltpu.VMEM((Z, PAIR, PAIR) + block, bf16),
        pltpu.VMEM((Z, PAIR, PAIR) + block, bf16),
        pltpu.VMEM((Z, PAIR) + block, bf16),
        pltpu.VMEM((Z, PAIR) + block, bf16),
        pltpu.VMEM((Z,) + block, bf16),
        pltpu.VMEM((Z,) + block, bf16),
        pltpu.VMEM((Z - 1,) + block, bf16),
        pltpu.VMEM((Z - 1,) + block, bf16),
        pltpu.VMEM((Z, PAIR, own, cols), bf16),
        pltpu.VMEM((4 * rows, cols), f32),
        pltpu.VMEM((3, rows, cols), f32),
        dma((Z, PAIR * PAIR)), dma, dma((PAIR, PAIR, Z)), dma((PAIR,)), dma((3,)),
        dma((PAIR, 3)), dma((PAIR, 3)),
        dma((Z,)), dma((Z,)), dma((Z,)), dma((Z,)), dma((Z,)), dma((Z,)),
        dma((Z - 1,)), dma((Z - 1,)),
        dma((Z - 1, 2)), dma((Z - 1, 2)), dma((Z, 2)), dma((Z, 2)), dma((3,)), dma((3,)),
    ]
    out_shape = (
        jax.ShapeDtypeStruct(master.shape, f32),
        jax.ShapeDtypeStruct(master.shape, f32),
        jax.ShapeDtypeStruct(master.shape, f32),
        jax.ShapeDtypeStruct((rows, cols), bf16),
    )
    results = pl.pallas_call(
        functools.partial(kernel, Z, own),
        out_shape=tuple(pltpu.VMEM(a.shape, a.dtype) for a in out_shape),
        in_specs=[hbm_spec] * 6,
        out_specs=(vmem_spec,) * 4,
        scratch_shapes=scratch,
        compiler_params=pltpu.CompilerParams(
            collective_id=0, has_side_effects=True, vmem_limit_bytes=VMEM_BYTES
        ),
    )(tokens_in, cotangent, next_tokens, master, first_moment, second_moment)
    return pl.pallas_call(
        write_out,
        out_shape=out_shape,
        in_specs=[vmem_spec] * 4,
        out_specs=(vmem_spec,) * 4,
        compiler_params=pltpu.CompilerParams(vmem_limit_bytes=VMEM_BYTES // 8),
    )(*results)


def plain(tokens_in, cotangent, next_tokens, master, first_moment, second_moment):
    n_rep = lax.axis_size("replica")
    n_shard = lax.axis_size("shard")
    model_width = tokens_in.shape[1]
    own_rows = model_width // (n_rep * n_shard)
    blocked = lax.psum_scatter(
        lax.dot_general(
            tokens_in, cotangent, (((0,), (0,)), ((), ())), preferred_element_type=jnp.float32
        ),
        "replica",
        scatter_dimension=0,
        tiled=True,
    )
    gradient = lax.psum_scatter(blocked, "shard", scatter_dimension=0, tiled=True)
    new_master, new_first, new_second = adam(gradient, master, first_moment, second_moment)
    low_weight = new_master.astype(jnp.bfloat16)
    group_rows = lax.all_gather(low_weight, "replica", axis=0, tiled=True)
    row_count = next_tokens.shape[0]
    arranged = next_tokens.reshape(row_count, n_rep, n_shard, own_rows).transpose(0, 2, 1, 3)
    columns = arranged.reshape(row_count, model_width)
    summed = jnp.dot(
        columns,
        lax.all_gather(group_rows, "shard", axis=0, tiled=True),
        preferred_element_type=jnp.float32,
    )
    return (new_master, new_first, new_second, summed.astype(jnp.bfloat16))


def solution(mesh):
    n_rep, n_shard = mesh.shape["replica"], mesh.shape["shard"]

    def on_device(tokens_in, cotangent, next_tokens, master, first_moment, second_moment):
        own, cols = master.shape
        fits = (
            n_rep == PAIR * PAIR
            and n_shard % PAIR == 0
            and n_shard // PAIR > 2
            and (n_shard // PAIR) & (n_shard // PAIR - 1) == 0
            and own % 256 == 0
            and cols % 128 == 0
            and next_tokens.shape[0] % 16 == 0
            and tokens_in.shape[0] % 128 == 0
        )
        args = (tokens_in, cotangent, next_tokens, master, first_moment, second_moment)
        if fits:
            return tuple(fused(n_shard // PAIR, *args))
        return plain(*args)

    spec = P(("replica", "shard"), None)
    return jax.shard_map(
        on_device, mesh=mesh, in_specs=(spec,) * 6, out_specs=(spec,) * 4, check_vma=False
    )
```

```python
import functools

import jax
import jax.numpy as jnp
from jax import lax
from jax.experimental import pallas as pl
from jax.experimental.pallas import tpu as pltpu
from jax.sharding import PartitionSpec as P

beta_one = 0.9
beta_two = 0.95
learn_rate = 0.003
decay_rate = 0.1
epsilon = 1e-08
steps_done = 10

MESH = pl.DeviceIdType.MESH
PAIR = 2
VMEM_BYTES = 62 * 2**20


def adam(gradient, master, first_moment, second_moment):
    new_first = beta_one * first_moment + (1.0 - beta_one) * gradient
    new_second = beta_two * second_moment + (1.0 - beta_two) * gradient * gradient
    first_hat = new_first / (1.0 - beta_one**steps_done)
    second_hat = new_second / (1.0 - beta_two**steps_done)
    new_master = master - learn_rate * (
        first_hat / (jnp.sqrt(second_hat) + epsilon) + decay_rate * master
    )
    return new_master, new_first, new_second


def kernel(
    Z, own,
    tok_hbm, cot_hbm, nxt_hbm, master_hbm, first_hbm, second_hbm,
    nm_out, nf_out, ns_out, out_ref,
    tok, cot, ntok, nxt, state,
    g32, gb, rc, hb, rp, jb, rq, kb, rz, wall, acc, ro,
    tok_sem, cot_sem, ntok_sem, nxt_sem, state_sem,
    n_s, n_r, c_s, c_r, p_s, p_r, q_s, q_r, z_s, z_r,
    az_s, az_r, aq_s, aq_r, o_s, o_r,
):
    f32, bf16 = jnp.float32, jnp.bfloat16
    r, s = lax.axis_index("replica"), lax.axis_index("shard")
    y, c, z, x = r // PAIR, r % PAIR, s // PAIR, s % PAIR
    p, q = x * (1 - c) + y * c, y * (1 - c) + x * c
    wide = PAIR * own
    rows = nxt_hbm.shape[0]

    def at(yy, cc, zz, xx):
        return (yy * PAIR + cc, zz * PAIR + xx)

    def over_p(cc):
        return at(y * (1 - c) + (1 - y) * c, cc, z, (1 - x) * (1 - c) + x * c)

    def over_q(cc):
        return at((1 - y) * (1 - c) + y * c, cc, z, x * (1 - c) + (1 - x) * c)

    def z_of(d):
        zz, bit = z, 1
        while bit < Z:
            if d & bit:
                zz = zz + bit - 2 * bit * ((zz // bit) % 2)
            bit *= 2
        return zz

    def z_at(d):
        return at(y, c, z_of(d), x)

    sib, p_peer, q_peer = at(y, 1 - c, z, x), over_p(c), over_q(c)

    barrier = pltpu.get_barrier_semaphore()
    peers = [sib, p_peer, q_peer, over_p(1 - c), over_q(1 - c)]
    peers += [z_at(j) for j in range(1, Z)]
    for d in peers:
        pl.semaphore_signal(barrier, inc=1, device_id=d, device_id_type=MESH)

    loads, ntok_loads = [], []
    cot_load = pltpu.make_async_copy(cot_hbm, cot, cot_sem)
    cot_load.start()
    for k in range(Z):
        zc = z_of(Z - 1 - k)
        row = []
        for yc in range(PAIR * PAIR):
            col = pl.multiple_of((yc * Z + zc) * wide, own)
            cp = pltpu.make_async_copy(
                tok_hbm.at[:, pl.ds(col, wide)], tok.at[k, yc], tok_sem.at[k, yc]
            )
            cp.start()
            row.append(cp)
        loads.append(row)
        if k == 0:
            for yy in range(PAIR):
                for h in range(PAIR):
                    for zz in range(Z):
                        cp = pltpu.make_async_copy(
                            nxt_hbm.at[:, pl.ds(((yy * PAIR + h) * Z + zz) * wide, wide)],
                            ntok.at[yy, h, zz], ntok_sem.at[yy, h, zz],
                        )
                        cp.start()
                        ntok_loads.append(cp)

    def send(src, dst, s_sem, r_sem, dev):
        cp = pltpu.make_async_remote_copy(
            src_ref=src, dst_ref=dst, send_sem=s_sem, recv_sem=r_sem,
            device_id=dev, device_id_type=MESH,
        )
        cp.start()
        return cp

    cot_load.wait()
    cot_t = cot[...].astype(f32).T.astype(bf16)
    core_cp, p_cp, q_cp, z_cp = {}, {}, {}, {}

    def term(k, h, yy, xx):
        return jnp.dot(
            cot_t, tok[k, yy * PAIR + h, :, xx * own:(xx + 1) * own],
            preferred_element_type=f32,
        )

    def place(h, yy, xx):
        return xx * (1 - h) + yy * h, yy * (1 - h) + xx * h

    def stage_core(k):
        for cp in loads[k]:
            cp.wait()
        for yy in range(PAIR):
            for xx in range(PAIR):
                gb[(k,) + place(1 - c, yy, xx)] = term(k, 1 - c, yy, xx).astype(bf16)
        if k == 0:
            pl.semaphore_wait(barrier, len(peers))
        core_cp[k] = send(gb.at[k], rc.at[k], c_s.at[k], c_r.at[k], sib)

    def own_terms(k):
        for yy in range(PAIR):
            for xx in range(PAIR):
                g32[(k,) + place(c, yy, xx)] = term(k, c, yy, xx)

    def stage_p(k):
        core_cp[k].wait_recv()
        for i, qq in enumerate((1 - q, q)):
            hb[k, i] = (g32[k, 1 - p, qq] + rc[k, 1 - p, qq].astype(f32)).astype(bf16)
            p_cp[k, i] = send(hb.at[k, i], rp.at[k, i], p_s.at[k, i], p_r.at[k, i], p_peer)

    def partial(k, i):
        qq = (1 - q, q)[i]
        p_cp[k, i].wait_recv()
        return g32[k, p, qq] + rc[k, p, qq].astype(f32) + rp[k, i].astype(f32)

    def stage_q(k):
        jb[k] = partial(k, 0).astype(bf16)
        q_cp[k] = send(jb.at[k], rq.at[k], q_s.at[k], q_r.at[k], q_peer)

    def stage_z(k):
        total = partial(k, 1)
        q_cp[k].wait_recv()
        total = total + rq[k].astype(f32)
        if k == Z - 1:
            return total
        kb[k] = total.astype(bf16)
        z_cp[k] = send(kb.at[k], rz.at[k], z_s.at[k], z_r.at[k], z_at(Z - 1 - k))
        return None

    swaps, nxt_loads = {}, {}

    def columns_for(h, pp, qq):
        yy, xx = qq * (1 - h) + pp * h, pp * (1 - h) + qq * h
        return ntok.at[yy, h, :, :, pl.ds(pl.multiple_of(xx * own, own), own)]

    def swap(i, who):
        h, pp, qq, dev = (
            (1 - c, q, p, sib), (c, 1 - p, q, p_peer), (1 - c, 1 - q, p, over_q(1 - c))
        )[who]
        qq = qq if i == 0 else 1 - qq
        swaps[i, who] = send(
            columns_for(h, pp, qq), nxt.at[qq, :, pl.ds((who + 1) * rows, rows)],
            n_s.at[i, who], n_r.at[i, who], dev,
        )

    def local_tokens(i):
        qq = q if i == 0 else 1 - q
        nxt_loads[i] = pltpu.make_async_copy(
            columns_for(c, p, qq), nxt.at[qq, :, pl.ds(0, rows)], nxt_sem.at[i]
        )
        nxt_loads[i].start()

    state_loads = [
        pltpu.make_async_copy(src, state.at[i], state_sem.at[i])
        for i, src in enumerate((master_hbm, first_hbm, second_hbm))
    ]
    total = None
    for t in range(Z + 4):
        if t < Z:
            stage_core(t)
            if t == 0:
                for cp in ntok_loads:
                    cp.wait()
                swap(0, 1)
                swap(0, 2)
        if 0 <= t - 1 < Z:
            stage_p(t - 1)
        if t < Z:
            own_terms(t)
        if t == 1:
            for cp in state_loads:
                cp.start()
        if t == Z:
            for i in range(PAIR):
                local_tokens(i)
                swap(i, 0)
        if 0 <= t - 3 < Z:
            stage_q(t - 3)
        if t == Z + 2:
            swap(1, 1)
            swap(1, 2)
        if 0 <= t - 4 < Z:
            total = stage_z(t - 4)

    for cp in state_loads:
        cp.wait()
    for k in range(Z - 1):
        z_cp[k].wait_recv()

    az, aq, stores = {}, {}, []
    half = own // 2

    def piece(zz, hh):
        return wall.at[zz, q, pl.ds(hh * half, half)]

    def forward(j, hh):
        part = piece(z_of(j), hh)
        aq[j, hh] = send(part, part, aq_s.at[j, hh], aq_r.at[j, hh], q_peer)

    for hh in range(2):
        part = pl.ds(hh * half, half)
        gradient = total[:, hh * half:(hh + 1) * half]
        for k in range(Z - 1):
            gradient = gradient + rz[k, :, part].astype(f32)
        new_master, new_first, new_second = adam(
            gradient.T, state[0, part], state[1, part], state[2, part]
        )
        wall[z, q, part] = new_master.astype(bf16)
        for j in range(Z - 1, 0, -1):
            az[j, hh] = send(
                piece(z, hh), piece(z, hh), az_s.at[j - 1, hh], az_r.at[j - 1, hh], z_at(j)
            )
        forward(0, hh)
        nm_out[part] = new_master
        nf_out[part] = new_first
        ns_out[part] = new_second

    def product(j, i, first, count):
        zj = z_of(j)
        qq = q if i == 0 else 1 - q
        return jnp.dot(
            nxt[qq, zj, pl.ds(first, count)], wall[zj, qq], preferred_element_type=f32
        )

    def tokens_here(i):
        nxt_loads[i].wait()
        for who in range(3):
            swaps[i, who].wait_recv()

    order = [0] + list(range(Z - 1, 0, -1))

    def second(n):
        for hh in range(2):
            aq[order[n], hh].wait_recv()
        return product(order[n], 1, 0, 4 * rows)

    for n in range(1, Z):
        for hh in range(2):
            az[order[n], hh].wait_recv()
            forward(order[n], hh)
        if n == 1:
            tokens_here(0)
            acc[...] = product(0, 0, 0, 4 * rows)
        if n == 2:
            tokens_here(1)
        acc[...] += product(order[n], 0, 0, 4 * rows)
        if n >= 2:
            acc[...] += second(n - 2)
    acc[...] += second(Z - 2)
    end = order[Z - 1]
    for hh in range(2):
        aq[end, hh].wait_recv()

    far, near = pl.ds(2 * rows, 2 * rows), pl.ds(0, 2 * rows)
    acc[far] += product(end, 1, 2 * rows, 2 * rows)

    def part_to(who, dev):
        return send(
            acc.at[pl.ds((who + 1) * rows, rows)], ro.at[who], o_s.at[who], o_r.at[who], dev
        )

    last = [part_to(1, p_peer), part_to(2, over_p(1 - c))]
    acc[near] += product(end, 1, 0, 2 * rows)
    last.append(part_to(0, sib))
    for cps in (core_cp, p_cp, q_cp, z_cp, az, aq, swaps):
        for cp in cps.values():
            cp.wait_send()
    for cp in last:
        cp.wait_recv()
    out_ref[...] = (acc[pl.ds(0, rows)] + ro[0] + ro[1] + ro[2]).astype(bf16)
    for cp in last:
        cp.wait_send()


def write_out(a, b, c, d, a_out, b_out, c_out, d_out):
    a_out[...] = a[...]
    b_out[...] = b[...]
    c_out[...] = c[...]
    d_out[...] = d[...]


def fused(Z, tokens_in, cotangent, next_tokens, master, first_moment, second_moment):
    f32, bf16 = jnp.float32, jnp.bfloat16
    own, cols = master.shape
    count = tokens_in.shape[0]
    rows = next_tokens.shape[0]
    dma = pltpu.SemaphoreType.DMA
    block = (cols, own)
    vmem_spec = pl.BlockSpec(memory_space=pltpu.VMEM)
    hbm_spec = pl.BlockSpec(memory_space=pltpu.HBM)
    scratch = [
        pltpu.VMEM((Z, PAIR * PAIR, count, PAIR * own), bf16),
        pltpu.VMEM((count, cols), bf16),
        pltpu.VMEM((PAIR, PAIR, Z, rows, PAIR * own), bf16),
        pltpu.VMEM((PAIR, Z, 4 * rows, own), bf16),
        pltpu.VMEM((3, own, cols), f32),
        pltpu.VMEM((Z, PAIR, PAIR) + block, f32),
        pltpu.VMEM((Z, PAIR, PAIR) + block, bf16),
        pltpu.VMEM((Z, PAIR, PAIR) + block, bf16),
        pltpu.VMEM((Z, PAIR) + block, bf16),
        pltpu.VMEM((Z, PAIR) + block, bf16),
        pltpu.VMEM((Z,) + block, bf16),
        pltpu.VMEM((Z,) + block, bf16),
        pltpu.VMEM((Z - 1,) + block, bf16),
        pltpu.VMEM((Z - 1,) + block, bf16),
        pltpu.VMEM((Z, PAIR, own, cols), bf16),
        pltpu.VMEM((4 * rows, cols), f32),
        pltpu.VMEM((3, rows, cols), f32),
        dma((Z, PAIR * PAIR)), dma, dma((PAIR, PAIR, Z)), dma((PAIR,)), dma((3,)),
        dma((PAIR, 3)), dma((PAIR, 3)),
        dma((Z,)), dma((Z,)), dma((Z, PAIR)), dma((Z, PAIR)), dma((Z,)), dma((Z,)),
        dma((Z - 1,)), dma((Z - 1,)),
        dma((Z - 1, 2)), dma((Z - 1, 2)), dma((Z, 2)), dma((Z, 2)), dma((3,)), dma((3,)),
    ]
    out_shape = (
        jax.ShapeDtypeStruct(master.shape, f32),
        jax.ShapeDtypeStruct(master.shape, f32),
        jax.ShapeDtypeStruct(master.shape, f32),
        jax.ShapeDtypeStruct((rows, cols), bf16),
    )
    results = pl.pallas_call(
        functools.partial(kernel, Z, own),
        out_shape=tuple(pltpu.VMEM(a.shape, a.dtype) for a in out_shape),
        in_specs=[hbm_spec] * 6,
        out_specs=(vmem_spec,) * 4,
        scratch_shapes=scratch,
        compiler_params=pltpu.CompilerParams(
            collective_id=0, has_side_effects=True, vmem_limit_bytes=VMEM_BYTES
        ),
    )(tokens_in, cotangent, next_tokens, master, first_moment, second_moment)
    return pl.pallas_call(
        write_out,
        out_shape=out_shape,
        in_specs=[vmem_spec] * 4,
        out_specs=(vmem_spec,) * 4,
        compiler_params=pltpu.CompilerParams(vmem_limit_bytes=VMEM_BYTES // 8),
    )(*results)


def plain(tokens_in, cotangent, next_tokens, master, first_moment, second_moment):
    n_rep = lax.axis_size("replica")
    n_shard = lax.axis_size("shard")
    model_width = tokens_in.shape[1]
    own_rows = model_width // (n_rep * n_shard)
    blocked = lax.psum_scatter(
        lax.dot_general(
            tokens_in, cotangent, (((0,), (0,)), ((), ())), preferred_element_type=jnp.float32
        ),
        "replica",
        scatter_dimension=0,
        tiled=True,
    )
    gradient = lax.psum_scatter(blocked, "shard", scatter_dimension=0, tiled=True)
    new_master, new_first, new_second = adam(gradient, master, first_moment, second_moment)
    low_weight = new_master.astype(jnp.bfloat16)
    group_rows = lax.all_gather(low_weight, "replica", axis=0, tiled=True)
    row_count = next_tokens.shape[0]
    arranged = next_tokens.reshape(row_count, n_rep, n_shard, own_rows).transpose(0, 2, 1, 3)
    columns = arranged.reshape(row_count, model_width)
    summed = jnp.dot(
        columns,
        lax.all_gather(group_rows, "shard", axis=0, tiled=True),
        preferred_element_type=jnp.float32,
    )
    return (new_master, new_first, new_second, summed.astype(jnp.bfloat16))


def solution(mesh):
    n_rep, n_shard = mesh.shape["replica"], mesh.shape["shard"]

    def on_device(tokens_in, cotangent, next_tokens, master, first_moment, second_moment):
        own, cols = master.shape
        fits = (
            n_rep == PAIR * PAIR
            and n_shard % PAIR == 0
            and n_shard // PAIR > 2
            and (n_shard // PAIR) & (n_shard // PAIR - 1) == 0
            and own % 256 == 0
            and cols % 128 == 0
            and next_tokens.shape[0] % 16 == 0
            and tokens_in.shape[0] % 128 == 0
        )
        args = (tokens_in, cotangent, next_tokens, master, first_moment, second_moment)
        if fits:
            return tuple(fused(n_shard // PAIR, *args))
        return plain(*args)

    spec = P(("replica", "shard"), None)
    return jax.shard_map(
        on_device, mesh=mesh, in_specs=(spec,) * 6, out_specs=(spec,) * 4, check_vma=False
    )
```

```python
import functools

import jax
import jax.numpy as jnp
from jax import lax
from jax.experimental import pallas as pl
from jax.experimental.pallas import tpu as pltpu
from jax.sharding import PartitionSpec as P

beta_one = 0.9
beta_two = 0.95
learn_rate = 0.003
decay_rate = 0.1
epsilon = 1e-08
steps_done = 10

MESH = pl.DeviceIdType.MESH
PAIR = 2
VMEM_BYTES = 62 * 2**20


def adam(gradient, master, first_moment, second_moment):
    new_first = beta_one * first_moment + (1.0 - beta_one) * gradient
    new_second = beta_two * second_moment + (1.0 - beta_two) * gradient * gradient
    first_hat = new_first / (1.0 - beta_one**steps_done)
    second_hat = new_second / (1.0 - beta_two**steps_done)
    new_master = master - learn_rate * (
        first_hat / (jnp.sqrt(second_hat) + epsilon) + decay_rate * master
    )
    return new_master, new_first, new_second


def kernel(
    Z, own,
    tok_hbm, cot_hbm, nxt_hbm, master_hbm, first_hbm, second_hbm,
    nm_out, nf_out, ns_out, out_ref,
    tok, cot, ntok, nxt, state,
    g32, gb, rc, hb, rp, jb, rq, kb, rz, wall, acc, ro,
    tok_sem, cot_sem, ntok_sem, nxt_sem, state_sem,
    n_s, n_r, c_s, c_r, p_s, p_r, q_s, q_r, z_s, z_r,
    az_s, az_r, aq_s, aq_r, o_s, o_r,
):
    f32, bf16 = jnp.float32, jnp.bfloat16
    r, s = lax.axis_index("replica"), lax.axis_index("shard")
    y, c, z, x = r // PAIR, r % PAIR, s // PAIR, s % PAIR
    p, q = x * (1 - c) + y * c, y * (1 - c) + x * c
    wide = PAIR * own
    rows = nxt_hbm.shape[0]

    def at(yy, cc, zz, xx):
        return (yy * PAIR + cc, zz * PAIR + xx)

    def over_p(cc):
        return at(y * (1 - c) + (1 - y) * c, cc, z, (1 - x) * (1 - c) + x * c)

    def over_q(cc):
        return at((1 - y) * (1 - c) + y * c, cc, z, x * (1 - c) + (1 - x) * c)

    def z_of(d):
        zz, bit = z, 1
        while bit < Z:
            if d & bit:
                zz = zz + bit - 2 * bit * ((zz // bit) % 2)
            bit *= 2
        return zz

    def z_at(d):
        return at(y, c, z_of(d), x)

    sib, p_peer, q_peer = at(y, 1 - c, z, x), over_p(c), over_q(c)

    barrier = pltpu.get_barrier_semaphore()
    peers = [sib, p_peer, q_peer, over_p(1 - c), over_q(1 - c)]
    peers += [z_at(j) for j in range(1, Z)]
    for d in peers:
        pl.semaphore_signal(barrier, inc=1, device_id=d, device_id_type=MESH)

    loads, ntok_loads = [], []
    cot_load = pltpu.make_async_copy(cot_hbm, cot, cot_sem)
    cot_load.start()
    for k in range(Z):
        zc = z_of(Z - 1 - k)
        row = []
        for yc in range(PAIR * PAIR):
            col = pl.multiple_of((yc * Z + zc) * wide, own)
            cp = pltpu.make_async_copy(
                tok_hbm.at[:, pl.ds(col, wide)], tok.at[k, yc], tok_sem.at[k, yc]
            )
            cp.start()
            row.append(cp)
        loads.append(row)
        if k == 0:
            for yy in range(PAIR):
                for h in range(PAIR):
                    for zz in range(Z):
                        cp = pltpu.make_async_copy(
                            nxt_hbm.at[:, pl.ds(((yy * PAIR + h) * Z + zz) * wide, wide)],
                            ntok.at[yy, h, zz], ntok_sem.at[yy, h, zz],
                        )
                        cp.start()
                        ntok_loads.append(cp)

    def send(src, dst, s_sem, r_sem, dev):
        cp = pltpu.make_async_remote_copy(
            src_ref=src, dst_ref=dst, send_sem=s_sem, recv_sem=r_sem,
            device_id=dev, device_id_type=MESH,
        )
        cp.start()
        return cp

    cot_load.wait()
    cot_t = cot[...].astype(f32).T.astype(bf16)
    core_cp, p_cp, q_cp, z_cp = {}, {}, {}, {}

    def term(k, h, yy, xx):
        return jnp.dot(
            cot_t, tok[k, yy * PAIR + h, :, xx * own:(xx + 1) * own],
            preferred_element_type=f32,
        )

    def place(h, yy, xx):
        return xx * (1 - h) + yy * h, yy * (1 - h) + xx * h

    def stage_core(k):
        for cp in loads[k]:
            cp.wait()
        for yy in range(PAIR):
            for xx in range(PAIR):
                gb[(k,) + place(1 - c, yy, xx)] = term(k, 1 - c, yy, xx).astype(bf16)
        if k == 0:
            pl.semaphore_wait(barrier, len(peers))
        core_cp[k] = send(gb.at[k], rc.at[k], c_s.at[k], c_r.at[k], sib)

    def own_terms(k):
        for yy in range(PAIR):
            for xx in range(PAIR):
                g32[(k,) + place(c, yy, xx)] = term(k, c, yy, xx)

    def stage_p(k):
        core_cp[k].wait_recv()
        for i, qq in enumerate((1 - q, q)):
            hb[k, i] = (g32[k, 1 - p, qq] + rc[k, 1 - p, qq].astype(f32)).astype(bf16)
            p_cp[k, i] = send(hb.at[k, i], rp.at[k, i], p_s.at[k, i], p_r.at[k, i], p_peer)

    def partial(k, i):
        qq = (1 - q, q)[i]
        p_cp[k, i].wait_recv()
        return g32[k, p, qq] + rc[k, p, qq].astype(f32) + rp[k, i].astype(f32)

    def stage_q(k):
        jb[k] = partial(k, 0).astype(bf16)
        q_cp[k] = send(jb.at[k], rq.at[k], q_s.at[k], q_r.at[k], q_peer)

    def stage_z(k):
        total = partial(k, 1)
        q_cp[k].wait_recv()
        total = total + rq[k].astype(f32)
        if k == Z - 1:
            return total
        kb[k] = total.astype(bf16)
        z_cp[k] = send(kb.at[k], rz.at[k], z_s.at[k], z_r.at[k], z_at(Z - 1 - k))
        return None

    swaps, nxt_loads = {}, {}

    def columns_for(h, pp, qq):
        yy, xx = qq * (1 - h) + pp * h, pp * (1 - h) + qq * h
        return ntok.at[yy, h, :, :, pl.ds(pl.multiple_of(xx * own, own), own)]

    def swap(i, who):
        h, pp, qq, dev = (
            (1 - c, q, p, sib), (c, 1 - p, q, p_peer), (1 - c, 1 - q, p, over_q(1 - c))
        )[who]
        qq = qq if i == 0 else 1 - qq
        swaps[i, who] = send(
            columns_for(h, pp, qq), nxt.at[qq, :, pl.ds((who + 1) * rows, rows)],
            n_s.at[i, who], n_r.at[i, who], dev,
        )

    def local_tokens(i):
        qq = q if i == 0 else 1 - q
        nxt_loads[i] = pltpu.make_async_copy(
            columns_for(c, p, qq), nxt.at[qq, :, pl.ds(0, rows)], nxt_sem.at[i]
        )
        nxt_loads[i].start()

    state_loads = [
        pltpu.make_async_copy(src, state.at[i], state_sem.at[i])
        for i, src in enumerate((master_hbm, first_hbm, second_hbm))
    ]
    total = None
    for t in range(Z + 4):
        if t < Z:
            stage_core(t)
            if t == 0:
                for cp in ntok_loads:
                    cp.wait()
                swap(0, 1)
                swap(0, 2)
        if 0 <= t - 1 < Z:
            stage_p(t - 1)
        if t < Z:
            own_terms(t)
        if t == 1:
            for cp in state_loads:
                cp.start()
        if t == Z:
            for i in range(PAIR):
                local_tokens(i)
                swap(i, 0)
        if 0 <= t - 3 < Z:
            stage_q(t - 3)
        if t == Z + 2:
            swap(1, 1)
            swap(1, 2)
        if 0 <= t - 4 < Z:
            total = stage_z(t - 4)

    for cp in state_loads:
        cp.wait()
    for k in range(Z - 1):
        z_cp[k].wait_recv()

    az, aq, stores = {}, {}, []
    half = own // 2

    def piece(zz, hh):
        return wall.at[zz, q, pl.ds(hh * half, half)]

    def forward(j, hh):
        part = piece(z_of(j), hh)
        aq[j, hh] = send(part, part, aq_s.at[j, hh], aq_r.at[j, hh], q_peer)

    for hh in range(2):
        part = pl.ds(hh * half, half)
        gradient = total[:, hh * half:(hh + 1) * half]
        for k in range(Z - 1):
            gradient = gradient + rz[k, :, part].astype(f32)
        new_master, new_first, new_second = adam(
            gradient.T, state[0, part], state[1, part], state[2, part]
        )
        wall[z, q, part] = new_master.astype(bf16)
        for j in range(Z - 1, 0, -1):
            az[j, hh] = send(
                piece(z, hh), piece(z, hh), az_s.at[j - 1, hh], az_r.at[j - 1, hh], z_at(j)
            )
        forward(0, hh)
        nm_out[part] = new_master
        nf_out[part] = new_first
        ns_out[part] = new_second

    def product(j, i, first, count):
        zj = z_of(j)
        qq = q if i == 0 else 1 - q
        return jnp.dot(
            nxt[qq, zj, pl.ds(first, count)], wall[zj, qq], preferred_element_type=f32
        )

    def tokens_here(i):
        nxt_loads[i].wait()
        for who in range(3):
            swaps[i, who].wait_recv()

    order = [0] + list(range(Z - 1, 0, -1))
    for cps in (core_cp, p_cp, q_cp, z_cp):
        for cp in cps.values():
            cp.wait_send()

    def second(n):
        for hh in range(2):
            aq[order[n], hh].wait_recv()
        return product(order[n], 1, 0, 4 * rows)

    for n in range(1, Z):
        for hh in range(2):
            az[order[n], hh].wait_recv()
            forward(order[n], hh)
        if n == 1:
            tokens_here(0)
            acc[...] = product(0, 0, 0, 4 * rows)
        if n == 2:
            tokens_here(1)
            for cp in swaps.values():
                cp.wait_send()
        acc[...] += product(order[n], 0, 0, 4 * rows)
        if n >= 2:
            acc[...] += second(n - 2)
    acc[...] += second(Z - 2)
    end = order[Z - 1]
    for hh in range(2):
        aq[end, hh].wait_recv()

    far, near = pl.ds(2 * rows, 2 * rows), pl.ds(0, 2 * rows)
    acc[far] += product(end, 1, 2 * rows, 2 * rows)

    def part_to(who, dev):
        return send(
            acc.at[pl.ds((who + 1) * rows, rows)], ro.at[who], o_s.at[who], o_r.at[who], dev
        )

    last = [part_to(1, p_peer), part_to(2, over_p(1 - c))]
    acc[near] += product(end, 1, 0, 2 * rows)
    last.append(part_to(0, sib))
    for cps in (az, aq):
        for cp in cps.values():
            cp.wait_send()
    for cp in last:
        cp.wait_recv()
    out_ref[...] = (acc[pl.ds(0, rows)] + ro[0] + ro[1] + ro[2]).astype(bf16)
    for cp in last:
        cp.wait_send()


def write_out(a, b, c, d, a_out, b_out, c_out, d_out):
    a_out[...] = a[...]
    b_out[...] = b[...]
    c_out[...] = c[...]
    d_out[...] = d[...]


def fused(Z, tokens_in, cotangent, next_tokens, master, first_moment, second_moment):
    f32, bf16 = jnp.float32, jnp.bfloat16
    own, cols = master.shape
    count = tokens_in.shape[0]
    rows = next_tokens.shape[0]
    dma = pltpu.SemaphoreType.DMA
    block = (cols, own)
    vmem_spec = pl.BlockSpec(memory_space=pltpu.VMEM)
    hbm_spec = pl.BlockSpec(memory_space=pltpu.HBM)
    scratch = [
        pltpu.VMEM((Z, PAIR * PAIR, count, PAIR * own), bf16),
        pltpu.VMEM((count, cols), bf16),
        pltpu.VMEM((PAIR, PAIR, Z, rows, PAIR * own), bf16),
        pltpu.VMEM((PAIR, Z, 4 * rows, own), bf16),
        pltpu.VMEM((3, own, cols), f32),
        pltpu.VMEM((Z, PAIR, PAIR) + block, f32),
        pltpu.VMEM((Z, PAIR, PAIR) + block, bf16),
        pltpu.VMEM((Z, PAIR, PAIR) + block, bf16),
        pltpu.VMEM((Z, PAIR) + block, bf16),
        pltpu.VMEM((Z, PAIR) + block, bf16),
        pltpu.VMEM((Z,) + block, bf16),
        pltpu.VMEM((Z,) + block, bf16),
        pltpu.VMEM((Z - 1,) + block, bf16),
        pltpu.VMEM((Z - 1,) + block, bf16),
        pltpu.VMEM((Z, PAIR, own, cols), bf16),
        pltpu.VMEM((4 * rows, cols), f32),
        pltpu.VMEM((3, rows, cols), f32),
        dma((Z, PAIR * PAIR)), dma, dma((PAIR, PAIR, Z)), dma((PAIR,)), dma((3,)),
        dma((PAIR, 3)), dma((PAIR, 3)),
        dma((Z,)), dma((Z,)), dma((Z, PAIR)), dma((Z, PAIR)), dma((Z,)), dma((Z,)),
        dma((Z - 1,)), dma((Z - 1,)),
        dma((Z - 1, 2)), dma((Z - 1, 2)), dma((Z, 2)), dma((Z, 2)), dma((3,)), dma((3,)),
    ]
    out_shape = (
        jax.ShapeDtypeStruct(master.shape, f32),
        jax.ShapeDtypeStruct(master.shape, f32),
        jax.ShapeDtypeStruct(master.shape, f32),
        jax.ShapeDtypeStruct((rows, cols), bf16),
    )
    results = pl.pallas_call(
        functools.partial(kernel, Z, own),
        out_shape=tuple(pltpu.VMEM(a.shape, a.dtype) for a in out_shape),
        in_specs=[hbm_spec] * 6,
        out_specs=(vmem_spec,) * 4,
        scratch_shapes=scratch,
        compiler_params=pltpu.CompilerParams(
            collective_id=0, has_side_effects=True, vmem_limit_bytes=VMEM_BYTES
        ),
    )(tokens_in, cotangent, next_tokens, master, first_moment, second_moment)
    return pl.pallas_call(
        write_out,
        out_shape=out_shape,
        in_specs=[vmem_spec] * 4,
        out_specs=(vmem_spec,) * 4,
        compiler_params=pltpu.CompilerParams(vmem_limit_bytes=VMEM_BYTES // 8),
    )(*results)


def plain(tokens_in, cotangent, next_tokens, master, first_moment, second_moment):
    n_rep = lax.axis_size("replica")
    n_shard = lax.axis_size("shard")
    model_width = tokens_in.shape[1]
    own_rows = model_width // (n_rep * n_shard)
    blocked = lax.psum_scatter(
        lax.dot_general(
            tokens_in, cotangent, (((0,), (0,)), ((), ())), preferred_element_type=jnp.float32
        ),
        "replica",
        scatter_dimension=0,
        tiled=True,
    )
    gradient = lax.psum_scatter(blocked, "shard", scatter_dimension=0, tiled=True)
    new_master, new_first, new_second = adam(gradient, master, first_moment, second_moment)
    low_weight = new_master.astype(jnp.bfloat16)
    group_rows = lax.all_gather(low_weight, "replica", axis=0, tiled=True)
    row_count = next_tokens.shape[0]
    arranged = next_tokens.reshape(row_count, n_rep, n_shard, own_rows).transpose(0, 2, 1, 3)
    columns = arranged.reshape(row_count, model_width)
    summed = jnp.dot(
        columns,
        lax.all_gather(group_rows, "shard", axis=0, tiled=True),
        preferred_element_type=jnp.float32,
    )
    return (new_master, new_first, new_second, summed.astype(jnp.bfloat16))


def solution(mesh):
    n_rep, n_shard = mesh.shape["replica"], mesh.shape["shard"]

    def on_device(tokens_in, cotangent, next_tokens, master, first_moment, second_moment):
        own, cols = master.shape
        fits = (
            n_rep == PAIR * PAIR
            and n_shard % PAIR == 0
            and n_shard // PAIR > 2
            and (n_shard // PAIR) & (n_shard // PAIR - 1) == 0
            and own % 256 == 0
            and cols % 128 == 0
            and next_tokens.shape[0] % 16 == 0
            and tokens_in.shape[0] % 128 == 0
        )
        args = (tokens_in, cotangent, next_tokens, master, first_moment, second_moment)
        if fits:
            return tuple(fused(n_shard // PAIR, *args))
        return plain(*args)

    spec = P(("replica", "shard"), None)
    return jax.shard_map(
        on_device, mesh=mesh, in_specs=(spec,) * 6, out_specs=(spec,) * 4, check_vma=False
    )
```
